512 devices in a mesh: section: 32 (over z_hi, y, core), expert: 4 (over z_lo), dp: 4 (over x).
Axes of the slice: x: 4, y: 8, z: 8 (z_hi: 2, z_lo: 4; z = z_hi * 4 + z_lo), core: 2. Of those that a mesh axis runs over, the one named last changes fastest.
Arguments:
- section_outputs: bfloat16 [32, 4, 512, 2048], P('section', 'dp', 'expert'), may hold values from -6 to 6
- first_tokens: bfloat16 [4, 512, 2048], P('dp', 'expert'), may hold values from -6 to 6
- kept_layer_inputs: bfloat16 [32, 4, 512, 2048], P('section', 'dp', 'expert'), may hold values from -6 to 6
- section_cotangents: bfloat16 [32, 4, 512, 2048], P('section', 'dp', 'expert'), may hold values from -6 to 6
- loss_cotangent: bfloat16 [4, 512, 2048], P('dp', 'expert'), may hold values from -6 to 6
- norm_gain: float32 [32, 2048], P('section'), may hold values from 0.5 to 1.5
- gate_weights: bfloat16 [32, 768, 2048], P('section', 'expert', 'dp'), may hold values from -0.125 to 0.125
- up_weights: bfloat16 [32, 768, 2048], P('section', 'expert', 'dp'), may hold values from -0.125 to 0.125
- down_weights: bfloat16 [32, 768, 2048], P('section', 'expert', 'dp'), may hold values from -0.21875 to 0.21875
- forward_experts: int32 [32, 4, 512, 8], P('section', 'dp', 'expert'), may hold values from 0 to 127, as said below
- forward_scales: float32 [32, 4, 512, 8], P('section', 'dp', 'expert'), may hold values from 0.05 to 0.6
- backward_experts: int32 [32, 4, 512, 8], P('section', 'dp', 'expert'), may hold values from 0 to 127, as said below
- backward_scales: float32 [32, 4, 512, 8], P('section', 'dp', 'expert'), may hold values from 0.05 to 0.6
Outputs:
- layer_outputs: bfloat16 [32, 4, 512, 2048], P('section', 'dp', 'expert')
- input_grads: bfloat16 [32, 4, 512, 2048], P('section', 'dp', 'expert')
- gate_grads: bfloat16 [32, 768, 2048], P('section', 'expert', 'dp')
- up_grads: bfloat16 [32, 768, 2048], P('section', 'expert', 'dp')
- down_grads: bfloat16 [32, 768, 2048], P('section', 'expert', 'dp')
- gain_grads: float32 [32, 2048], P('section')
The draws below stay inside these ranges and needn't reach their ends.
Inputs may be any that keep to these rules, and one draw needn't show every extreme that they name: `forward_experts`: each token names 8 different experts. Expert 0 is named by at most 48 of the 128 tokens of one sequence shard; in every draw all 4 shards of some micro-batch of one replica at one section reach 48. `backward_experts`: each token names 8 different experts. Expert 0 is named by at most 48 of the 128 tokens of one sequence shard; in every draw all 4 shards of some micro-batch of one replica at one section reach 48.
All inputs are finite; a program needn't handle non-finite values.
Results may differ from the reference program's by a relative error of at most 0.013.
Values may be sent and summed in bfloat16 or wider, within the bound.
A program may use at most 64 MiB of HBM per device.

```python
import math
import jax
import jax.numpy as jnp
from jax import lax

D = 2048
FF = 768
EXPERTS = 128
TOP = 8
TOK_DEV = 128
CAP = 48
SEQ = 512
SECTIONS = 32
REPLICAS = 4
SHARDS = 4


def routing(key):
    load_key, section_key, replica_key, order_key, others_key, position_key = jax.random.split(key, 6)
    block_loads = jax.random.randint(load_key, (SECTIONS, REPLICAS, SHARDS), CAP // 4, CAP + 1)
    full_section = jax.random.randint(section_key, (), 0, SECTIONS)
    full_replica = jax.random.randint(replica_key, (), 0, REPLICAS)
    filled = (jnp.arange(SECTIONS)[:, None, None] == full_section) & (jnp.arange(REPLICAS)[None, :, None] == full_replica)
    block_loads = jnp.where(filled, CAP, block_loads)
    scores = jax.random.randint(order_key, (SECTIONS, REPLICAS, SHARDS, TOK_DEV), 0, 2 ** 20) * TOK_DEV + jnp.arange(TOK_DEV)
    ranking = jnp.argsort(jnp.argsort(scores, axis=-1), axis=-1)
    routed = (ranking < block_loads[..., None]).reshape(SECTIONS, REPLICAS, SEQ)
    others = jax.random.randint(others_key, (SECTIONS, REPLICAS, SEQ, EXPERTS - 1), 0, 2 ** 20) * (EXPERTS - 1) + jnp.arange(EXPERTS - 1)
    unused, picked = lax.top_k(others, TOP)
    chosen = picked + 1
    position = jax.random.randint(position_key, (SECTIONS, REPLICAS, SEQ, 1), 0, TOP)
    chosen = jnp.where(routed[..., None] & (jnp.arange(TOP) == position), 0, chosen)
    return chosen.astype(jnp.int32)


def draw_forward_experts(key, part):
    key = jax.random.fold_in(key, 11)
    return routing(key)


def draw_backward_experts(key, part):
    key = jax.random.fold_in(key, 23)
    return routing(key)


def block_levels(stream_key, shape, cuts, least, largest):
    def one(axis_at, parts):
        steps = jax.random.uniform(jax.random.fold_in(jax.random.fold_in(stream_key, 6), axis_at), (parts,), jnp.float32, least / len(cuts), largest / len(cuts))
        return jnp.repeat(jnp.exp(steps), shape[axis_at] // parts).reshape((-1,) + (1,) * (len(shape) - axis_at - 1))

    level = one(*cuts[0])
    for cut in cuts[1:]:
        level = level * one(*cut)
    return level


def normal_values(own_key, shape, spread, limit, cuts=(), kind=jnp.bfloat16):
    entries = jax.random.normal(own_key, shape, jnp.float32) * spread
    if len(cuts) > 0:
        entries = block_levels(own_key, shape, cuts, -0.22, 0.18) * entries
    return jnp.clip(entries, min=-limit, max=limit).astype(kind)


def setup_inputs(seed: int = 0) -> dict:
    seeds = jax.random.split(jax.random.key(seed), 14)
    return {
        "section_outputs": normal_values(seeds[0], (SECTIONS, REPLICAS, SEQ, D), 1.0, 6.0, ((0, 32), (1, 4), (2, 4))),
        "first_tokens": normal_values(seeds[1], (REPLICAS, SEQ, D), 1.0, 6.0, ((0, 4), (1, 4))),
        "kept_layer_inputs": normal_values(seeds[2], (SECTIONS, REPLICAS, SEQ, D), 1.0, 6.0, ((0, 32), (1, 4), (2, 4))),
        "section_cotangents": normal_values(seeds[3], (SECTIONS, REPLICAS, SEQ, D), 1.0, 6.0, ((0, 32), (1, 4), (2, 4))),
        "loss_cotangent": normal_values(seeds[4], (REPLICAS, SEQ, D), 1.0, 6.0, ((0, 4), (1, 4))),
        "norm_gain": jnp.clip(1.0 + 0.1 * jax.random.normal(seeds[5], (SECTIONS, D), jnp.float32), 0.5, 1.5),
        "gate_weights": normal_values(seeds[6], (SECTIONS, FF, D), D ** -0.5, 0.125, ((0, 32), (1, 4), (2, 4))),
        "up_weights": normal_values(seeds[7], (SECTIONS, FF, D), D ** -0.5, 0.125, ((0, 32), (1, 4), (2, 4))),
        "down_weights": normal_values(seeds[8], (SECTIONS, FF, D), FF ** -0.5, 0.21875, ((0, 32), (1, 4), (2, 4))),
        "forward_experts": draw_forward_experts(jax.random.fold_in(seeds[13], 71), 0),
        "forward_scales": jnp.clip(jnp.exp(math.log(0.6) - 2.4849067 * jax.random.uniform(seeds[10], (SECTIONS, REPLICAS, SEQ, TOP), jnp.float32) ** block_levels(seeds[10], (SECTIONS, REPLICAS, SEQ, TOP), ((0, 32), (1, 4), (2, 4)), -0.2, 0.2)), 0.05, 0.6),
        "backward_experts": draw_backward_experts(jax.random.fold_in(seeds[13], 71), 0),
        "backward_scales": jnp.clip(jnp.exp(math.log(0.6) - 2.4849067 * jax.random.uniform(seeds[12], (SECTIONS, REPLICAS, SEQ, TOP), jnp.float32) ** block_levels(seeds[12], (SECTIONS, REPLICAS, SEQ, TOP), ((0, 32), (1, 4), (2, 4)), -0.2, 0.2)), 0.05, 0.6),
    }


epsilon = 1e-06

def root_square_normalise(values, norm_scale_vector):
    broadened_value = values.astype(jnp.float32)
    inverse_root_scale = lax.rsqrt(lax.optimization_barrier(jnp.mean(broadened_value * broadened_value, axis=-1, keepdims=True)) + epsilon)
    unit_input_rows = broadened_value * inverse_root_scale
    return (unit_input_rows, inverse_root_scale, (unit_input_rows * norm_scale_vector).astype(jnp.bfloat16))

def tables(chosen, weights):
    picked = chosen == 0
    routed = jnp.any(picked, axis=-1)
    slot_index = jnp.cumsum(routed.astype(jnp.int32), axis=-1) - 1
    places = jnp.arange(CAP, dtype=jnp.int32)
    routing_table = ((slot_index[..., None, :] == places[:, None]) & routed[..., None, :]).astype(jnp.float32)
    route_scale = lax.optimization_barrier(jnp.sum(jnp.where(picked, weights, jnp.zeros_like(weights)), axis=-1))
    return (routing_table, route_scale)

def rounded(values):
    return lax.optimization_barrier(values.astype(jnp.bfloat16)).astype(jnp.float32)

def layer_step(section_items):
    layer_input_rows, kept_input_rows, cot_in, norm_scale_vector, gate_w, lift_w, down_w, ids_ahead, wts_ahead, ids_behind, wts_behind = section_items
    block = (REPLICAS, SHARDS, TOK_DEV)
    fdev = FF // SHARDS
    gate_f = gate_w.astype(jnp.float32)
    lift_f = lift_w.astype(jnp.float32)
    down_f = down_w.astype(jnp.float32)

    def quarters(values, weight):
        split_vals = values.astype(jnp.float32).reshape(REPLICAS, SHARDS * CAP, SHARDS, fdev)
        return jnp.einsum('rnqf,qfd->rqnd', split_vals, weight.reshape(SHARDS, fdev, D))

    def gather_rows(routing_table, values):
        picked_rows = jnp.einsum('recT,reTd->recd', routing_table, values.astype(jnp.float32))
        return picked_rows.astype(jnp.bfloat16).reshape(REPLICAS, SHARDS * CAP, D)

    def spread_rows(routing_table, values):
        return jnp.einsum('recT,recd->reTd', routing_table, values.reshape(REPLICAS, SHARDS, CAP, D), precision=lax.Precision.HIGHEST)

    def projections(rows_in):
        broadened_value = rows_in.astype(jnp.float32)
        return (jnp.einsum('rnd,fd->rnf', broadened_value, gate_f), jnp.einsum('rnd,fd->rnf', broadened_value, lift_f))
    layer_input_rows = layer_input_rows.reshape(block + (D,))
    unit_input_rows, inverse_root_scale, normalised_rows = root_square_normalise(layer_input_rows, norm_scale_vector)
    routing_table, route_scale = tables(ids_ahead.reshape(block + (TOP,)), wts_ahead.reshape(block + (TOP,)))
    rows_in = gather_rows(routing_table, normalised_rows)
    gate_act, up_act = projections(rows_in)
    hidden = (jax.nn.silu(gate_act) * up_act).astype(jnp.bfloat16)
    expert_out = lax.optimization_barrier(jnp.sum(rounded(quarters(hidden, down_f)), axis=1))
    expert_tokens = spread_rows(routing_table, expert_out)
    layer_out = (layer_input_rows.astype(jnp.float32) + route_scale[..., None] * expert_tokens).astype(jnp.bfloat16)
    kept_input_rows = kept_input_rows.reshape(block + (D,))
    cotangent_broad = cot_in.reshape(block + (D,)).astype(jnp.float32)
    unit_input_rows_back, inverse_root_scale_back, normalised_rows_back = root_square_normalise(kept_input_rows, norm_scale_vector)
    table_b, scale_b = tables(ids_behind.reshape(block + (TOP,)), wts_behind.reshape(block + (TOP,)))
    scaled = (scale_b[..., None] * cotangent_broad).astype(jnp.bfloat16)
    rows_back = gather_rows(table_b, normalised_rows_back)
    rows_grad = gather_rows(table_b, scaled)
    gate_act, up_act = projections(rows_back)
    squash = jax.nn.sigmoid(gate_act)
    hidden_b = (gate_act * squash * up_act).astype(jnp.bfloat16)
    grad_hidden = jnp.einsum('rnd,fd->rnf', rows_grad.astype(jnp.float32), down_f)
    grad_gate = (grad_hidden * up_act * squash * (1.0 + gate_act * (1.0 - squash))).astype(jnp.bfloat16)
    grad_lift = (grad_hidden * gate_act * squash).astype(jnp.bfloat16)
    grad_normed = lax.optimization_barrier(jnp.sum(rounded(quarters(grad_gate, gate_f) + quarters(grad_lift, lift_f)), axis=1))
    normalised_tokens = spread_rows(table_b, grad_normed)
    scale_vector_gradient = lax.optimization_barrier(jnp.sum(normalised_tokens * unit_input_rows_back, axis=(0, 1, 2)))
    unit_input_gradient = normalised_tokens * norm_scale_vector
    inner_product_mean = lax.optimization_barrier(jnp.mean(unit_input_gradient * unit_input_rows_back, axis=-1, keepdims=True))
    input_gradient = (cotangent_broad + inverse_root_scale_back * (unit_input_gradient - unit_input_rows_back * inner_product_mean)).astype(jnp.bfloat16)

    def replica_sum(former, latter):
        per_replica = jnp.einsum('rnf,rnd->rfd', former.astype(jnp.float32), latter.astype(jnp.float32))
        return lax.optimization_barrier(jnp.sum(rounded(per_replica), axis=0)).astype(jnp.bfloat16)
    return (layer_out.reshape(REPLICAS, SEQ, D), input_gradient.reshape(REPLICAS, SEQ, D), replica_sum(grad_gate, rows_back), replica_sum(grad_lift, rows_back), replica_sum(hidden_b, rows_grad), scale_vector_gradient)

def reference(section_outputs, first_tokens, kept_layer_inputs, section_cotangents, loss_cotangent, norm_gain, gate_weights, up_weights, down_weights, forward_experts, forward_scales, backward_experts, backward_scales):
    arriving_gradient = jnp.concatenate([first_tokens[None], section_outputs[:-1]], axis=0)
    cotangent = jnp.concatenate([section_cotangents[1:], loss_cotangent[None]], axis=0)
    results = lax.map(layer_step, (arriving_gradient, kept_layer_inputs, cotangent, norm_gain, gate_weights, up_weights, down_weights, forward_experts, forward_scales, backward_experts, backward_scales))
    return (results[0], results[1], results[2], results[3], results[4], results[5])
```

```python
import jax
import jax.numpy as jnp
from jax import lax
from jax.experimental import pallas as pl
from jax.experimental.pallas import tpu as pltpu
from jax.sharding import PartitionSpec as P

CAP = 48
TOK = 128
D = 2048
HID = 192
DS = 512
EPS = 1e-06
MESH = pl.DeviceIdType.MESH
BF = jnp.bfloat16
F32 = jnp.float32


def dot_tt(a, b):
    return lax.dot_general(a, b, (((0,), (0,)), ((), ())), preferred_element_type=F32)


def dot_nt(a, b):
    return lax.dot_general(a, b, (((1,), (1,)), ((), ())), preferred_element_type=F32)


def dot_nn(a, b):
    return jnp.dot(a, b, preferred_element_type=F32)


def tables(chosen, weights):
    picked = chosen == 0
    routed = jnp.max(picked.astype(F32), axis=1, keepdims=True)
    scale = jnp.sum(jnp.where(picked, weights, 0.0), axis=1, keepdims=True)
    row = lax.broadcasted_iota(jnp.int32, (TOK, TOK), 0)
    col = lax.broadcasted_iota(jnp.int32, (TOK, TOK), 1)
    lower = (col <= row).astype(BF)
    count = dot_nn(lower, jnp.broadcast_to(routed, (TOK, TOK)).astype(BF))[:, :1]
    slot = jnp.where(routed > 0.5, count - 1.0, -1.0)
    place = lax.broadcasted_iota(jnp.int32, (TOK, 4 * CAP), 1)
    place = (
        place
        - CAP * (place >= CAP).astype(jnp.int32)
        - CAP * (place >= 2 * CAP).astype(jnp.int32)
        - CAP * (place >= 3 * CAP).astype(jnp.int32)
    )
    table = jnp.where(slot == place.astype(F32), 1.0, 0.0).astype(BF)
    return table, scale


def inverse_rms(x):
    return lax.rsqrt(jnp.mean(x * x, axis=1, keepdims=True) + EPS)


def sigmoid(v):
    return 1.0 / (1.0 + jnp.exp(-v))


def kernel(
    so_ref, ft_ref, kept_ref, sc_ref, lc_ref, gain_ref, gw_ref, uw_ref, dw_ref, fe_ref, fs_ref, be_ref, bs_ref,
    lo_ref, ig_ref, gg_ref, ug_ref, dg_ref, gt_ref,
    kept, cot, inc, w, rows, part, got, dwst, dwgot, dwout, lo, ig, gst, gout,
    lsem, osem, ssem, srsem, wsend, wrecv, zsend, zrecv, psend, precv, dsend, drecv, gsend, grecv,
):
    s, e, r = lax.axis_index("section"), lax.axis_index("expert"), lax.axis_index("dp")
    last = lax.axis_size("section") - 1
    inner = (e == 1) | (e == 2)
    outer = jnp.logical_not(inner)
    end = jnp.where(e == 1, 0, 3)
    other = 3 - e
    far = 3 - end
    near = jnp.where(e == 0, 1, 2)

    def remote(src, dst, ss, rs, dev):
        return pltpu.make_async_remote_copy(
            src_ref=src, dst_ref=dst, send_sem=ss, recv_sem=rs, device_id=dev, device_id_type=MESH
        )

    xs = [lax.rem(r + d, 4) for d in range(4)]
    zs = [lax.rem(e + d, 4) for d in range(4)]

    own_w = [pltpu.make_async_copy(ref, w.at[a, r], lsem.at[1 + a]) for a, ref in enumerate((gw_ref, uw_ref, dw_ref))]
    load_kept = pltpu.make_async_copy(kept_ref, kept, lsem.at[0])
    load_kept.start()
    barrier = pltpu.get_barrier_semaphore()
    for d in (1, 2, 3):
        pl.semaphore_signal(barrier, inc=1, device_id=(s, e, xs[d]), device_id_type=MESH)
        pl.semaphore_signal(barrier, inc=1, device_id=(s, zs[d], r), device_id_type=MESH)

    @pl.when(s < last)
    def _():
        pl.semaphore_signal(barrier, inc=1, device_id=(s + 1, e, r), device_id_type=MESH)

    @pl.when(s > 0)
    def _():
        pl.semaphore_signal(barrier, inc=1, device_id=(s - 1, e, r), device_id_type=MESH)

    for c in own_w:
        c.start()
    first_in = pltpu.make_async_copy(ft_ref, inc, lsem.at[4])
    loss_in = pltpu.make_async_copy(lc_ref, cot, lsem.at[5])

    @pl.when(s == 0)
    def _():
        first_in.start()

    @pl.when(s == last)
    def _():
        loss_in.start()

    pl.semaphore_wait(barrier, 6 + jnp.where((s > 0) & (s < last), 2, 1))

    hop_cot = remote(sc_ref, cot, ssem.at[0], srsem.at[0], (jnp.maximum(s - 1, 0), e, r))
    hop_inc = remote(so_ref, inc, ssem.at[1], srsem.at[1], (jnp.minimum(s + 1, last), e, r))

    @pl.when(s > 0)
    def _():
        hop_cot.start()

    @pl.when(s < last)
    def _():
        hop_inc.start()

    w_copies = []
    for a, ref in enumerate((gw_ref, uw_ref, dw_ref)):
        for d in (1, 3, 2):
            c = remote(ref, w.at[a, r], wsend.at[a, d], wrecv.at[a, d], (s, e, xs[d]))
            c.start()
            w_copies.append(c)

    def z_copy(a, block, k, dev):
        return remote(rows.at[a, block], rows.at[a, block], zsend.at[a, k], zrecv.at[a, block], (s, dev, r))

    def z_own(a):
        @pl.when(inner)
        def _():
            z_copy(a, e, 0, other).start()
            z_copy(a, e, 1, end).start()

        @pl.when(outer)
        def _():
            z_copy(a, e, 0, near).start()

    def z_pass(a, block, k, dev):
        @pl.when(inner)
        def _():
            c = z_copy(a, block, k, dev)
            c.wait_recv()
            c.start()

    gain = gain_ref[...]
    load_kept.wait()
    x = kept[...].astype(F32)
    rscale_b = inverse_rms(x)
    table_b, scale_b = tables(be_ref[...], bs_ref[...])
    pick_b = table_b[:, :CAP]
    rows[0, e] = dot_tt(pick_b, (x * rscale_b * gain).astype(BF)).astype(BF)
    z_own(0)
    table_f, scale_f = tables(fe_ref[...], fs_ref[...])
    z_pass(0, end, 2, other)
    z_pass(0, other, 3, end)

    @pl.when(s == last)
    def _():
        loss_in.wait()

    @pl.when(s < last)
    def _():
        hop_cot.wait_recv()

    rows[1, e] = dot_tt(pick_b, (scale_b * cot[...].astype(F32)).astype(BF)).astype(BF)
    z_own(1)

    @pl.when(s == 0)
    def _():
        first_in.wait()

    @pl.when(s > 0)
    def _():
        hop_inc.wait_recv()

    y = inc[...].astype(F32)
    rows[2, e] = dot_tt(table_f[:, :CAP], (y * inverse_rms(y) * gain).astype(BF)).astype(BF)

    @pl.when(outer)
    def _():
        z_copy(2, e, 0, near).start()

    z_pass(0, far, 4, end)
    z_pass(1, end, 2, other)
    z_pass(1, other, 3, end)

    @pl.when(inner)
    def _():
        z_copy(2, e, 0, other).start()

    z_pass(1, far, 4, end)

    @pl.when(inner)
    def _():
        z_copy(2, e, 1, end).start()

    z_pass(2, end, 2, other)
    z_pass(2, other, 3, end)
    z_pass(2, far, 4, end)

    def z_arrived(a):
        @pl.when(outer)
        def _():
            for d in (1, 2, 3):
                z_copy(a, zs[d], 0, near).wait_recv()

    def w_arrived(a):
        own_w[a].wait()
        for c in w_copies[3 * a : 3 * a + 3]:
            c.wait_recv()

    def project(a, group):
        total = None
        for k in range(4):
            term = dot_nt(group[:, k * DS : (k + 1) * DS], w[a, k])
            total = term if total is None else total + term
        return total

    def send_parts(j):
        for d in (1, 2, 3):
            remote(part.at[j, zs[d]], got.at[j, e], psend.at[j, d], precv.at[j, d], (s, zs[d], r)).start()
        got[j, e] = part[j, e]

    def parts_arrived(j):
        for d in (1, 2, 3):
            c = remote(part.at[j, zs[d]], got.at[j, e], psend.at[j, d], precv.at[j, d], (s, zs[d], r))
            c.wait()

    z_arrived(0)
    w_arrived(0)
    w_arrived(1)
    group_in = rows[0].reshape(4 * CAP, D)
    gate_act = project(0, group_in)
    up_act = project(1, group_in)
    squash = sigmoid(gate_act)
    act = gate_act * squash
    hidden_b = (act * up_act).astype(BF)
    z_arrived(1)
    w_arrived(2)
    group_grad = rows[1].reshape(4 * CAP, D)
    grad_hidden = project(2, group_grad)
    grad_gate = (grad_hidden * up_act * squash * (1.0 + gate_act * (1.0 - squash))).astype(BF)
    grad_up = (grad_hidden * act).astype(BF)
    for k in range(4):
        cols = slice(k * DS, (k + 1) * DS)
        term = dot_nn(grad_gate, w[0, k]) + dot_nn(grad_up, w[1, k])
        part[0, :, :, cols] = term.astype(BF).reshape(4, CAP, DS)
    send_parts(0)

    d_copies = []
    for a, (left, right) in enumerate(((grad_gate, group_in), (grad_up, group_in), (hidden_b, group_grad))):
        for k in range(4):
            dwst[a, k] = dot_tt(left, right[:, k * DS : (k + 1) * DS]).astype(BF)
        for d in (1, 3, 2):
            c = remote(dwst.at[a, xs[d]], dwgot.at[a, r], dsend.at[a, d], drecv.at[a, d], (s, e, xs[d]))
            c.start()
            d_copies.append(c)

    z_arrived(2)
    group = rows[2].reshape(4 * CAP, D)
    g = project(0, group)
    u = project(1, group)
    hidden = (g * sigmoid(g) * u).astype(BF)
    for k in range(4):
        cols = slice(k * DS, (k + 1) * DS)
        part[1, :, :, cols] = dot_nn(hidden, w[2, k]).astype(BF).reshape(4, CAP, DS)
    send_parts(1)

    parts_arrived(0)
    grad_normed = dot_nn(table_b, got[0].reshape(4 * CAP, D))
    xhat = kept[...].astype(F32) * rscale_b
    gst[0, 0] = jnp.sum(grad_normed * xhat, axis=0, keepdims=True)
    gain_z = []
    for d in (1, 2, 3):
        c = remote(gst.at[0, 0], gst.at[0, d], gsend.at[0, d], grecv.at[0, d], (s, zs[d], r))
        c.start()
        gain_z.append(c)
    gx = grad_normed * gain
    mean = jnp.mean(gx * xhat, axis=1, keepdims=True)
    ig[...] = (cot[...].astype(F32) + rscale_b * (gx - xhat * mean)).astype(BF)
    out_ig = pltpu.make_async_copy(ig, ig_ref, osem.at[0])
    out_ig.start()
    for c in gain_z:
        c.wait_recv()
    gst[1, 0] = (gst[0, 0] + gst[0, 1]) + (gst[0, 2] + gst[0, 3])
    gain_x = []
    for d in (1, 2, 3):
        c = remote(gst.at[1, 0], gst.at[1, d], gsend.at[1, d], grecv.at[1, d], (s, e, xs[d]))
        c.start()
        gain_x.append(c)

    parts_arrived(1)
    tokens = dot_nn(table_f, got[1].reshape(4 * CAP, D))
    lo[...] = (inc[...].astype(F32) + scale_f * tokens).astype(BF)
    out_lo = pltpu.make_async_copy(lo, lo_ref, osem.at[1])
    out_lo.start()
    outs = [out_ig, out_lo]

    for a, ref in enumerate((gg_ref, ug_ref, dg_ref)):
        total = dwst[a, r].astype(F32)
        for d in (1, 2, 3):
            d_copies[3 * a + (0, 0, 2, 1)[d]].wait_recv()
        for d in (1, 2, 3):
            total = total + dwgot[a, xs[d]].astype(F32)
        dwout[a] = total.astype(BF)
        c = pltpu.make_async_copy(dwout.at[a], ref, osem.at[2 + a])
        c.start()
        outs.append(c)
    for c in gain_x:
        c.wait_recv()
    gout[...] = (gst[1, 0] + gst[1, 1]) + (gst[1, 2] + gst[1, 3])
    c = pltpu.make_async_copy(gout, gt_ref, osem.at[5])
    c.start()
    outs.append(c)

    @pl.when(s > 0)
    def _():
        hop_cot.wait_send()

    @pl.when(s < last)
    def _():
        hop_inc.wait_send()

    for c in w_copies + d_copies + gain_z + gain_x:
        c.wait_send()
    for a in range(3):
        z_copy(a, e, 0, near).wait_send()

        @pl.when(inner)
        def _():
            for k in range(1, 5):
                z_copy(a, e, k, end).wait_send()

    for c in outs:
        c.wait()


def local(so, ft, kept, sc, lc, gain, gw, uw, dw, fe, fs, be, bs):
    any_spec = pl.BlockSpec(memory_space=pl.ANY)
    vm = pl.BlockSpec(memory_space=pltpu.VMEM)
    dma = pltpu.SemaphoreType.DMA
    outs = pl.pallas_call(
        kernel,
        out_shape=(
            jax.ShapeDtypeStruct((TOK, D), BF),
            jax.ShapeDtypeStruct((TOK, D), BF),
            jax.ShapeDtypeStruct((HID, DS), BF),
            jax.ShapeDtypeStruct((HID, DS), BF),
            jax.ShapeDtypeStruct((HID, DS), BF),
            jax.ShapeDtypeStruct((1, D), F32),
        ),
        in_specs=[any_spec] * 5 + [vm] + [any_spec] * 3 + [vm] * 4,
        out_specs=[any_spec] * 6,
        scratch_shapes=[
            pltpu.VMEM((TOK, D), BF),
            pltpu.VMEM((TOK, D), BF),
            pltpu.VMEM((TOK, D), BF),
            pltpu.VMEM((3, 4, HID, DS), BF),
            pltpu.VMEM((3, 4, CAP, D), BF),
            pltpu.VMEM((2, 4, CAP, D), BF),
            pltpu.VMEM((2, 4, CAP, D), BF),
            pltpu.VMEM((3, 4, HID, DS), BF),
            pltpu.VMEM((3, 4, HID, DS), BF),
            pltpu.VMEM((3, HID, DS), BF),
            pltpu.VMEM((TOK, D), BF),
            pltpu.VMEM((TOK, D), BF),
            pltpu.VMEM((2, 4, 1, D), F32),
            pltpu.VMEM((1, D), F32),
            dma((6,)),
            dma((6,)),
            dma((2,)),
            dma((2,)),
            dma((3, 4)),
            dma((3, 4)),
            dma((3, 5)),
            dma((3, 4)),
            dma((2, 4)),
            dma((2, 4)),
            dma((3, 4)),
            dma((3, 4)),
            dma((2, 4)),
            dma((2, 4)),
        ],
        compiler_params=pltpu.CompilerParams(
            collective_id=0, has_side_effects=True, vmem_limit_bytes=40 << 20
        ),
        name="relay",
    )(
        so.reshape(TOK, D), ft.reshape(TOK, D), kept.reshape(TOK, D), sc.reshape(TOK, D), lc.reshape(TOK, D),
        gain.reshape(1, D), gw[0], uw[0], dw[0], fe[0, 0], fs[0, 0], be[0, 0], bs[0, 0],
    )
    return (
        outs[0][None, None], outs[1][None, None], outs[2][None], outs[3][None], outs[4][None], outs[5],
    )


def solution(mesh):
    tokens = P("section", "dp", "expert", None)
    stored = P("section", "expert", "dp")
    first = P("dp", "expert", None)
    return jax.shard_map(
        local,
        mesh=mesh,
        in_specs=(tokens, first, tokens, tokens, first, P("section", None)) + (stored,) * 3 + (tokens,) * 4,
        out_specs=(tokens, tokens, stored, stored, stored, P("section", None)),
        check_vma=False,
    )
```

```python
import jax
import jax.numpy as jnp
from jax import lax
from jax.experimental import pallas as pl
from jax.experimental.pallas import tpu as pltpu
from jax.sharding import PartitionSpec as P

CAP = 48
TOK = 128
D = 2048
HID = 192
DS = 512
EPS = 1e-06
CA = 3
CR = 3
MESH = pl.DeviceIdType.MESH
BF = jnp.bfloat16
F32 = jnp.float32


def dot_tt(a, b):
    return lax.dot_general(a, b, (((0,), (0,)), ((), ())), preferred_element_type=F32)


def dot_nt(a, b):
    return lax.dot_general(a, b, (((1,), (1,)), ((), ())), preferred_element_type=F32)


def dot_nn(a, b):
    return jnp.dot(a, b, preferred_element_type=F32)


def tables(chosen, weights):
    chosen, weights = chosen.T, weights.T
    picked = chosen == 0
    routed = jnp.max(picked.astype(F32), axis=1, keepdims=True)
    scale = jnp.sum(jnp.where(picked, weights, 0.0), axis=1, keepdims=True)
    row = lax.broadcasted_iota(jnp.int32, (TOK, TOK), 0)
    col = lax.broadcasted_iota(jnp.int32, (TOK, TOK), 1)
    lower = (col <= row).astype(BF)
    count = dot_nn(lower, jnp.broadcast_to(routed, (TOK, TOK)).astype(BF))[:, :1]
    slot = jnp.where(routed > 0.5, count - 1.0, -1.0)
    place = lax.broadcasted_iota(jnp.int32, (TOK, 4 * CAP), 1)
    place = (
        place
        - CAP * (place >= CAP).astype(jnp.int32)
        - CAP * (place >= 2 * CAP).astype(jnp.int32)
        - CAP * (place >= 3 * CAP).astype(jnp.int32)
    )
    table = jnp.where(slot == place.astype(F32), 1.0, 0.0).astype(BF)
    return table, scale


def inverse_rms(x):
    return lax.rsqrt(jnp.mean(x * x, axis=1, keepdims=True) + EPS)


def sigmoid(v):
    return 1.0 / (1.0 + jnp.exp(-v))


def kernel(
    so_ref, ft_ref, kept_ref, sc_ref, lc_ref, gain_ref, gw_ref, uw_ref, dw_ref, fe_ref, fs_ref, be_ref, bs_ref,
    lo_ref, ig_ref, gg_ref, ug_ref, dg_ref, gt_ref,
    kept, cot, inc, w, rows, part, got, mid, relay, dwst, dwgot, dwout, lo, ig, gst, gout,
    lsem, osem, ssem, srsem, wsend, wrecv, zsend, zrecv, psend, precv, csend, crecv, rsem, dsend, drecv, gsend, grecv,
):
    s, e, r = lax.axis_index("section"), lax.axis_index("expert"), lax.axis_index("dp")
    last = lax.axis_size("section") - 1
    inner = (e == 1) | (e == 2)
    outer = jnp.logical_not(inner)
    end = jnp.where(e == 1, 0, 3)
    other = 3 - e
    far = 3 - end
    near = jnp.where(e == 0, 1, 2)

    def remote(src, dst, ss, rs, dev):
        return pltpu.make_async_remote_copy(
            src_ref=src, dst_ref=dst, send_sem=ss, recv_sem=rs, device_id=dev, device_id_type=MESH
        )

    xs = [lax.rem(r + d, 4) for d in range(4)]
    zs = [lax.rem(e + d, 4) for d in range(4)]

    own_w = [pltpu.make_async_copy(ref, w.at[a, r], lsem.at[1 + a]) for a, ref in enumerate((gw_ref, uw_ref, dw_ref))]
    load_kept = pltpu.make_async_copy(kept_ref, kept, lsem.at[0])
    load_kept.start()
    barrier = pltpu.get_barrier_semaphore()
    for d in (1, 2, 3):
        pl.semaphore_signal(barrier, inc=1, device_id=(s, e, xs[d]), device_id_type=MESH)
        pl.semaphore_signal(barrier, inc=1, device_id=(s, zs[d], r), device_id_type=MESH)

    from_next = (s < last) & (s != last // 2)
    from_before = (s > 0) & (s != last // 2 + 1)

    @pl.when(from_next)
    def _():
        pl.semaphore_signal(barrier, inc=1, device_id=(s + 1, e, r), device_id_type=MESH)

    @pl.when(from_before)
    def _():
        pl.semaphore_signal(barrier, inc=1, device_id=(s - 1, e, r), device_id_type=MESH)

    half = (last + 1) // 2
    relays = half // 2
    up_relay = (s > half) & (lax.rem(s, 2) == 1)
    down_relay = (s < half) & (lax.rem(s, 2) == 0)
    relay_at = jnp.where(s > half, s - half, s) // 2

    @pl.when(up_relay)
    def _():
        pl.semaphore_signal(barrier, inc=1, device_id=(half - 1, e, r), device_id_type=MESH)

    @pl.when(down_relay)
    def _():
        pl.semaphore_signal(barrier, inc=1, device_id=(half, e, r), device_id_type=MESH)

    @pl.when(s == half)
    def _():
        for k in range(relays):
            pl.semaphore_signal(barrier, inc=1, device_id=(half + 1 + 2 * k, e, r), device_id_type=MESH)

    @pl.when(s == half - 1)
    def _():
        for k in range(relays):
            pl.semaphore_signal(barrier, inc=1, device_id=(2 * k, e, r), device_id_type=MESH)

    for c in own_w:
        c.start()
    first_in = pltpu.make_async_copy(ft_ref, inc, lsem.at[4])
    loss_in = pltpu.make_async_copy(lc_ref, cot, lsem.at[5])

    @pl.when(s == 0)
    def _():
        first_in.start()

    @pl.when(s == last)
    def _():
        loss_in.start()

    one, none = jnp.int32(1), jnp.int32(0)
    pl.semaphore_wait(
        barrier,
        6
        + jnp.where(from_next, one, none)
        + jnp.where(from_before, one, none)
        + jnp.where(up_relay | down_relay, one, none)
        + jnp.where((s == half) | (s == half - 1), relays, 0),
    )

    hop_cot = remote(sc_ref, cot, ssem.at[0], srsem.at[0], (jnp.maximum(s - 1, 0), e, r))
    hop_inc = remote(so_ref, inc, ssem.at[1], srsem.at[1], (jnp.minimum(s + 1, last), e, r))

    @pl.when(from_before)
    def _():
        hop_cot.start()

    @pl.when(from_next)
    def _():
        hop_inc.start()

    step = TOK // relays

    def out_by(ref, k, section):
        return remote(ref.at[pl.ds(k * step, step)], relay, csend.at[k], rsem.at[0], (section, e, r))

    @pl.when(s == half - 1)
    def _():
        for k in range(relays):
            out_by(so_ref, k, half + 1 + 2 * k).start()

    @pl.when(s == half)
    def _():
        for k in range(relays):
            out_by(sc_ref, k, 2 * k).start()

    def in_by(dst, k, section):
        first = k * step if isinstance(k, int) else pl.multiple_of(k * step, step)
        return remote(relay, dst.at[pl.ds(first, step)], rsem.at[1], crecv.at[k], (section, e, r))

    def pass_relay():
        @pl.when(up_relay)
        def _():
            c = in_by(inc, relay_at, half)
            out_by(so_ref, 0, half).wait_recv()
            c.start()

        @pl.when(down_relay)
        def _():
            c = in_by(cot, relay_at, half - 1)
            out_by(sc_ref, 0, half).wait_recv()
            c.start()

    w_copies = []
    for a, ref in enumerate((gw_ref, uw_ref, dw_ref)):
        for d in (1, 3, 2):
            c = remote(ref, w.at[a, r], wsend.at[a, d], wrecv.at[a, d], (s, e, xs[d]))
            c.start()
            w_copies.append(c)

    ca = CAP // CA

    def z_copy(a, block, k, dev, c):
        ref = rows.at[a, block, pl.ds(c * ca, ca)]
        return remote(ref, ref, zsend.at[a, k, c], zrecv.at[a, block, c], (s, dev, r))

    def z_send(a, k, dev):
        for c in range(CA):
            z_copy(a, e, k, dev, c).start()

    def z_own(a):
        @pl.when(inner)
        def _():
            for c in range(CA):
                z_copy(a, e, 0, other, c).start()
                z_copy(a, e, 1, end, c).start()

        @pl.when(outer)
        def _():
            z_send(a, 0, near)

    def z_pass(a, *moves):
        @pl.when(inner)
        def _():
            for c in range(CA):
                for block, k, dev in moves:
                    copy = z_copy(a, block, k, dev, c)
                    copy.wait_recv()
                    copy.start()

    gain = gain_ref[...]
    load_kept.wait()
    x = kept[...].astype(F32)
    rscale_b = inverse_rms(x)
    table_b, scale_b = tables(be_ref[...], bs_ref[...])
    pick_b = table_b[:, :CAP]
    rows[0, e] = dot_tt(pick_b, (x * rscale_b * gain).astype(BF)).astype(BF)
    z_own(0)
    table_f, scale_f = tables(fe_ref[...], fs_ref[...])
    z_pass(0, (end, 2, other), (other, 3, end))
    pass_relay()

    @pl.when(s == last)
    def _():
        loss_in.wait()

    @pl.when(s == half - 1)
    def _():
        for k in range(relays):
            in_by(cot, k, half - 1).wait_recv()

    @pl.when(from_next)
    def _():
        hop_cot.wait_recv()

    rows[1, e] = dot_tt(pick_b, (scale_b * cot[...].astype(F32)).astype(BF)).astype(BF)
    z_own(1)

    @pl.when(s == 0)
    def _():
        first_in.wait()

    @pl.when(s == half)
    def _():
        for k in range(relays):
            in_by(inc, k, half).wait_recv()

    @pl.when(from_before)
    def _():
        hop_inc.wait_recv()

    y = inc[...].astype(F32)
    rows[2, e] = dot_tt(table_f[:, :CAP], (y * inverse_rms(y) * gain).astype(BF)).astype(BF)

    @pl.when(outer)
    def _():
        z_send(2, 0, near)

    z_pass(0, (far, 4, end))
    z_pass(1, (end, 2, other), (other, 3, end))

    @pl.when(inner)
    def _():
        z_send(2, 0, other)

    z_pass(1, (far, 4, end))

    @pl.when(inner)
    def _():
        z_send(2, 1, end)

    z_pass(2, (end, 2, other), (other, 3, end))
    z_pass(2, (far, 4, end))

    def z_arrived(a):
        @pl.when(outer)
        def _():
            for d in (1, 2, 3):
                for c in range(CA):
                    z_copy(a, zs[d], 0, near, c).wait_recv()

    def w_arrived(a):
        own_w[a].wait()
        for c in w_copies[3 * a : 3 * a + 3]:
            c.wait_recv()

    def project(a, group):
        total = None
        for k in range(4):
            term = dot_nt(group[:, k * DS : (k + 1) * DS], w[a, k])
            total = term if total is None else total + term
        return total

    cr = CAP // CR

    def leg(j, src, dst, k, m, dev, c):
        return remote(src, dst.at[pl.ds(c * cr, cr)], psend.at[j, k, c], precv.at[j, m, c], (s, dev, r))

    def for_far(j, c):
        return leg(j, part.at[j, 3 - e, pl.ds(c * cr, cr)], mid.at[j, 0], 0, 0, near, c)

    def for_across(j, c):
        return leg(j, part.at[j, 3 - near, pl.ds(c * cr, cr)], mid.at[j, 1], 1, 1, near, c)

    def for_near(j, c):
        return leg(j, part.at[j, near, pl.ds(c * cr, cr)], got.at[j, 1], 2, 2, near, c)

    def on_far(j, c):
        return leg(j, part.at[j, far, pl.ds(c * cr, cr)], mid.at[j, 2], 0, 3, other, c)

    def on_other(j, c):
        return leg(j, part.at[j, other, pl.ds(c * cr, cr)], got.at[j, 2], 1, 4, other, c)

    def on_end(j, c):
        return leg(j, part.at[j, end, pl.ds(c * cr, cr)], got.at[j, 1], 2, 2, end, c)

    def add_mid(j, dest, m, c):
        here = pl.ds(c * cr, cr)
        part[j, dest, here, :] = (part[j, dest, here, :].astype(F32) + mid[j, m, here, :].astype(F32)).astype(BF)

    def send_parts(j):
        got[j, 0] = part[j, e]

        @pl.when(outer)
        def _():
            got[j, 2] = jnp.zeros((CAP, D), BF)
            for make in (for_far, for_across, for_near):
                for c in range(CR):
                    make(j, c).start()

    def pass_parts(j):
        @pl.when(inner)
        def _():
            for c in range(CR):
                for_far(j, c).wait_recv()
                add_mid(j, far, 0, c)
                on_far(j, c).start()
            for c in range(CR):
                for_across(j, c).wait_recv()
                add_mid(j, other, 1, c)
                on_other(j, c).start()
            for c in range(CR):
                on_far(j, c).wait_recv()
                add_mid(j, end, 2, c)
                on_end(j, c).start()

    def parts_arrived(j):
        for c in range(CR):
            for_near(j, c).wait_recv()

        @pl.when(inner)
        def _():
            for c in range(CR):
                on_other(j, c).wait_recv()

    def parts_sent(j):
        for k in range(3):
            for c in range(CR):
                leg(j, part.at[j, 0, pl.ds(c * cr, cr)], mid.at[j, 0], k, 0, near, c).wait_send()

    z_arrived(0)
    w_arrived(0)
    w_arrived(1)
    group_in = rows[0].reshape(4 * CAP, D)
    gate_act = project(0, group_in)
    up_act = project(1, group_in)
    squash = sigmoid(gate_act)
    act = gate_act * squash
    hidden_b = (act * up_act).astype(BF)
    z_arrived(1)
    w_arrived(2)
    group_grad = rows[1].reshape(4 * CAP, D)
    grad_hidden = project(2, group_grad)
    grad_gate = (grad_hidden * up_act * squash * (1.0 + gate_act * (1.0 - squash))).astype(BF)
    grad_up = (grad_hidden * act).astype(BF)
    for k in range(4):
        cols = slice(k * DS, (k + 1) * DS)
        term = dot_nn(grad_gate, w[0, k]) + dot_nn(grad_up, w[1, k])
        part[0, :, :, cols] = term.astype(BF).reshape(4, CAP, DS)
    send_parts(0)

    d_copies = []
    for a, (left, right) in enumerate(((grad_gate, group_in), (grad_up, group_in), (hidden_b, group_grad))):
        for k in range(4):
            dwst[a, k] = dot_tt(left, right[:, k * DS : (k + 1) * DS]).astype(BF)
        for d in (1, 3, 2):
            c = remote(dwst.at[a, xs[d]], dwgot.at[a, r], dsend.at[a, d], drecv.at[a, d], (s, e, xs[d]))
            c.start()
            d_copies.append(c)

    z_arrived(2)
    group = rows[2].reshape(4 * CAP, D)
    g = project(0, group)
    u = project(1, group)
    hidden = (g * sigmoid(g) * u).astype(BF)
    for k in range(4):
        cols = slice(k * DS, (k + 1) * DS)
        part[1, :, :, cols] = dot_nn(hidden, w[2, k]).astype(BF).reshape(4, CAP, DS)
    send_parts(1)

    pass_parts(0)
    parts_arrived(0)
    grad_normed = dot_nn(table_b[:, : 3 * CAP], got[0].reshape(3 * CAP, D))
    xhat = kept[...].astype(F32) * rscale_b
    gst[0, 0] = jnp.sum(grad_normed * xhat, axis=0, keepdims=True)
    gain_z = []
    for d in (1, 2, 3):
        c = remote(gst.at[0, 0], gst.at[0, d], gsend.at[0, d], grecv.at[0, d], (s, zs[d], r))
        c.start()
        gain_z.append(c)
    gx = grad_normed * gain
    mean = jnp.mean(gx * xhat, axis=1, keepdims=True)
    ig[...] = (cot[...].astype(F32) + rscale_b * (gx - xhat * mean)).astype(BF)
    out_ig = pltpu.make_async_copy(ig, ig_ref, osem.at[0])
    out_ig.start()
    pass_parts(1)
    for c in gain_z:
        c.wait_recv()
    gst[1, 0] = (gst[0, 0] + gst[0, 1]) + (gst[0, 2] + gst[0, 3])
    gain_x = []
    for d in (1, 2, 3):
        c = remote(gst.at[1, 0], gst.at[1, d], gsend.at[1, d], grecv.at[1, d], (s, e, xs[d]))
        c.start()
        gain_x.append(c)

    parts_arrived(1)
    tokens = dot_nn(table_f[:, : 3 * CAP], got[1].reshape(3 * CAP, D))
    lo[...] = (inc[...].astype(F32) + scale_f * tokens).astype(BF)
    out_lo = pltpu.make_async_copy(lo, lo_ref, osem.at[1])
    out_lo.start()
    outs = [out_ig, out_lo]

    for a, ref in enumerate((gg_ref, ug_ref, dg_ref)):
        total = dwst[a, r].astype(F32)
        for d in (1, 2, 3):
            d_copies[3 * a + (0, 0, 2, 1)[d]].wait_recv()
        for d in (1, 2, 3):
            total = total + dwgot[a, xs[d]].astype(F32)
        dwout[a] = total.astype(BF)
        c = pltpu.make_async_copy(dwout.at[a], ref, osem.at[2 + a])
        c.start()
        outs.append(c)
    for c in gain_x:
        c.wait_recv()
    gout[...] = (gst[1, 0] + gst[1, 1]) + (gst[1, 2] + gst[1, 3])
    c = pltpu.make_async_copy(gout, gt_ref, osem.at[5])
    c.start()
    outs.append(c)

    @pl.when(from_before)
    def _():
        hop_cot.wait_send()

    @pl.when(from_next)
    def _():
        hop_inc.wait_send()

    @pl.when((s == half) | (s == half - 1))
    def _():
        for k in range(relays):
            out_by(so_ref, k, half).wait_send()

    @pl.when(up_relay | down_relay)
    def _():
        in_by(inc, 0, half).wait_send()

    parts_sent(0)
    parts_sent(1)

    for c in w_copies + d_copies + gain_z + gain_x:
        c.wait_send()
    for a in range(3):
        for c in range(CA):
            z_copy(a, e, 0, near, c).wait_send()

        @pl.when(inner)
        def _():
            for k in range(1, 5):
                for c in range(CA):
                    z_copy(a, e, k, end, c).wait_send()

    for c in outs:
        c.wait()


def finish(*refs):
    ins, outs, held, sems = refs[:6], refs[6:12], refs[12:18], refs[18]
    loads = [pltpu.make_async_copy(ins[i], held[i], sems.at[0, i]) for i in range(6)]
    stores = [pltpu.make_async_copy(held[i], outs[i], sems.at[1, i]) for i in range(6)]
    for c in loads:
        c.start()
    for load, store in zip(loads, stores):
        load.wait()
        store.start()
    for c in stores:
        c.wait()


def local(so, ft, kept, sc, lc, gain, gw, uw, dw, fe, fs, be, bs):
    any_spec = pl.BlockSpec(memory_space=pl.ANY)
    vm = pl.BlockSpec(memory_space=pltpu.VMEM)
    dma = pltpu.SemaphoreType.DMA
    outs = pl.pallas_call(
        kernel,
        out_shape=(
            jax.ShapeDtypeStruct((TOK, D), BF),
            jax.ShapeDtypeStruct((TOK, D), BF),
            jax.ShapeDtypeStruct((HID, DS), BF),
            jax.ShapeDtypeStruct((HID, DS), BF),
            jax.ShapeDtypeStruct((HID, DS), BF),
            jax.ShapeDtypeStruct((1, D), F32),
        ),
        in_specs=[any_spec] * 5 + [vm] + [any_spec] * 3 + [vm] * 4,
        out_specs=[any_spec] * 6,
        scratch_shapes=[
            pltpu.VMEM((TOK, D), BF),
            pltpu.VMEM((TOK, D), BF),
            pltpu.VMEM((TOK, D), BF),
            pltpu.VMEM((3, 4, HID, DS), BF),
            pltpu.VMEM((3, 4, CAP, D), BF),
            pltpu.VMEM((2, 4, CAP, D), BF),
            pltpu.VMEM((2, 3, CAP, D), BF),
            pltpu.VMEM((2, 3, CAP, D), BF),
            pltpu.VMEM((16, D), BF),
            pltpu.VMEM((3, 4, HID, DS), BF),
            pltpu.VMEM((3, 4, HID, DS), BF),
            pltpu.VMEM((3, HID, DS), BF),
            pltpu.VMEM((TOK, D), BF),
            pltpu.VMEM((TOK, D), BF),
            pltpu.VMEM((2, 4, 1, D), F32),
            pltpu.VMEM((1, D), F32),
            dma((6,)),
            dma((6,)),
            dma((2,)),
            dma((2,)),
            dma((3, 4)),
            dma((3, 4)),
            dma((3, 5, CA)),
            dma((3, 4, CA)),
            dma((2, 3, CR)),
            dma((2, 5, CR)),
            dma((8,)),
            dma((8,)),
            dma((2,)),
            dma((3, 4)),
            dma((3, 4)),
            dma((2, 4)),
            dma((2, 4)),
        ],
        compiler_params=pltpu.CompilerParams(
            collective_id=0, has_side_effects=True, vmem_limit_bytes=60 << 20
        ),
        name="relay",
    )(
        so.reshape(TOK, D), ft.reshape(TOK, D), kept.reshape(TOK, D), sc.reshape(TOK, D), lc.reshape(TOK, D),
        gain.reshape(1, D), gw[0], uw[0], dw[0], fe[0, 0].T, fs[0, 0].T, be[0, 0].T, bs[0, 0].T,
    )
    outs = pl.pallas_call(
        finish,
        out_shape=tuple(jax.ShapeDtypeStruct(o.shape, o.dtype) for o in outs),
        in_specs=[any_spec] * 6,
        out_specs=[any_spec] * 6,
        scratch_shapes=[pltpu.VMEM(o.shape, o.dtype) for o in outs] + [dma((2, 6))],
        compiler_params=pltpu.CompilerParams(vmem_limit_bytes=60 << 20),
        name="finish",
    )(*outs)
    return (
        outs[0][None, None], outs[1][None, None], outs[2][None], outs[3][None], outs[4][None], outs[5],
    )


def solution(mesh):
    tokens = P("section", "dp", "expert", None)
    stored = P("section", "expert", "dp")
    first = P("dp", "expert", None)
    return jax.shard_map(
        local,
        mesh=mesh,
        in_specs=(tokens, first, tokens, tokens, first, P("section", None)) + (stored,) * 3 + (tokens,) * 4,
        out_specs=(tokens, tokens, stored, stored, stored, P("section", None)),
        check_vma=False,
    )
```

```python
import jax
import jax.numpy as jnp
from jax import lax
from jax.experimental import pallas as pl
from jax.experimental.pallas import tpu as pltpu
from jax.sharding import PartitionSpec as P

CAP = 48
TOP = 8
TOK = 128
D = 2048
HID = 192
DS = 512
EPS = 1e-06
CA = 3
CR = 3
MESH = pl.DeviceIdType.MESH
BF = jnp.bfloat16
F32 = jnp.float32


def dot_tt(a, b):
    return lax.dot_general(a, b, (((0,), (0,)), ((), ())), preferred_element_type=F32)


def dot_nt(a, b):
    return lax.dot_general(a, b, (((1,), (1,)), ((), ())), preferred_element_type=F32)


def dot_nn(a, b):
    return jnp.dot(a, b, preferred_element_type=F32)


def tables(chosen, weights):
    chosen, weights = chosen.T, weights.T
    picked = chosen == 0
    routed = jnp.max(picked.astype(F32), axis=1, keepdims=True)
    scale = jnp.sum(jnp.where(picked, weights, 0.0), axis=1, keepdims=True)
    row = lax.broadcasted_iota(jnp.int32, (TOK, TOK), 0)
    col = lax.broadcasted_iota(jnp.int32, (TOK, TOK), 1)
    lower = (col <= row).astype(BF)
    count = dot_nn(lower, jnp.broadcast_to(routed, (TOK, TOK)).astype(BF))[:, :1]
    slot = jnp.where(routed > 0.5, count - 1.0, -1.0)
    place = lax.broadcasted_iota(jnp.int32, (TOK, 4 * CAP), 1)
    place = (
        place
        - CAP * (place >= CAP).astype(jnp.int32)
        - CAP * (place >= 2 * CAP).astype(jnp.int32)
        - CAP * (place >= 3 * CAP).astype(jnp.int32)
    )
    table = jnp.where(slot == place.astype(F32), 1.0, 0.0).astype(BF)
    return table, scale


def slots(chosen, weights):
    picked = chosen == 0
    routed = jnp.max(picked.astype(F32), axis=0, keepdims=True)
    scale = jnp.sum(jnp.where(picked, weights, 0.0), axis=0, keepdims=True)
    row = lax.broadcasted_iota(jnp.int32, (TOK, TOK), 0)
    col = lax.broadcasted_iota(jnp.int32, (TOK, TOK), 1)
    upper = (row <= col).astype(BF)
    count = dot_nn(jnp.broadcast_to(routed, (TOP, TOK)).astype(BF), upper)[:1]
    slot = jnp.where(routed > 0.5, count - 1.0, -1.0)
    hit = slot == lax.broadcasted_iota(jnp.int32, (CAP, TOK), 0).astype(F32)
    return jnp.where(hit, 1.0, 0.0).astype(BF), jnp.sum(jnp.where(hit, scale, 0.0), axis=1, keepdims=True)


def inverse_rms(x):
    return lax.rsqrt(jnp.mean(x * x, axis=1, keepdims=True) + EPS)


def sigmoid(v):
    return 1.0 / (1.0 + jnp.exp(-v))


def kernel(
    so_ref, ft_ref, kept_ref, sc_ref, lc_ref, gain_in, gw_ref, uw_ref, dw_ref, fe_in, fs_in, be_in, bs_in,
    lo_ref, ig_ref, gg_ref, ug_ref, dg_ref, gt_ref,
    fe_ref, fs_ref, be_ref, bs_ref, gain_ref, kept, cot, inc, w, rows, part, got, mid, relay, acts, dwst, dwmid, dwgot, dwout, lo, ig, gst, gout,
    lsem, osem, ssem, srsem, wsend, wrecv, zsend, zrecv, psend, precv, csend, crecv, rsem, ready, dsend, drecv, gsend, grecv,
):
    s, e, r = lax.axis_index("section"), lax.axis_index("expert"), lax.axis_index("dp")
    last = lax.axis_size("section") - 1
    inner = (e == 1) | (e == 2)
    outer = jnp.logical_not(inner)
    end = jnp.where(e == 1, 0, 3)
    other = 3 - e
    far = 3 - end
    near = jnp.where(e == 0, 1, 2)

    def remote(src, dst, ss, rs, dev):
        return pltpu.make_async_remote_copy(
            src_ref=src, dst_ref=dst, send_sem=ss, recv_sem=rs, device_id=dev, device_id_type=MESH
        )

    xs = [lax.rem(r + d, 4) for d in range(4)]
    zs = [lax.rem(e + d, 4) for d in range(4)]

    own_w = [pltpu.make_async_copy(ref, w.at[a, r], lsem.at[1 + a]) for a, ref in enumerate((gw_ref, uw_ref, dw_ref))]
    load_kept = pltpu.make_async_copy(kept_ref, kept, lsem.at[0])
    smalls = [
        pltpu.make_async_copy(src, dst, lsem.at[6 + i])
        for i, (src, dst) in enumerate(
            ((be_in, be_ref), (bs_in, bs_ref), (gain_in, gain_ref), (fe_in, fe_ref), (fs_in, fs_ref))
        )
    ]
    smalls[0].start()
    smalls[1].start()
    load_kept.start()
    for c in smalls[2:]:
        c.start()
    barrier = pltpu.get_barrier_semaphore()
    for d in (1, 3):
        pl.semaphore_signal(barrier, inc=1, device_id=(s, e, xs[d]), device_id_type=MESH)

    @pl.when(outer)
    def _():
        pl.semaphore_signal(barrier, inc=1, device_id=(s, near, r), device_id_type=MESH)

    @pl.when(inner)
    def _():
        pl.semaphore_signal(barrier, inc=1, device_id=(s, other, r), device_id_type=MESH)
        pl.semaphore_signal(barrier, inc=1, device_id=(s, end, r), device_id_type=MESH)

    from_next = (s < last) & (s != last // 2)
    from_before = (s > 0) & (s != last // 2 + 1)

    @pl.when(from_next)
    def _():
        pl.semaphore_signal(barrier, inc=1, device_id=(s + 1, e, r), device_id_type=MESH)

    @pl.when(from_before)
    def _():
        pl.semaphore_signal(barrier, inc=1, device_id=(s - 1, e, r), device_id_type=MESH)

    half = (last + 1) // 2
    relays = half // 2
    up_relay = (s > half) & (lax.rem(s, 2) == 1)
    down_relay = (s < half) & (lax.rem(s, 2) == 0)
    relay_at = jnp.where(s > half, s - half, s) // 2

    @pl.when(down_relay)
    def _():
        pl.semaphore_signal(barrier, inc=1, device_id=(half, e, r), device_id_type=MESH)

    @pl.when(s == half)
    def _():
        for k in range(relays):
            pl.semaphore_signal(barrier, inc=1, device_id=(half + 1 + 2 * k, e, r), device_id_type=MESH)

    @pl.when(s == half - 1)
    def _():
        for k in range(relays):
            pl.semaphore_signal(barrier, inc=1, device_id=(2 * k, e, r), device_id_type=MESH)
            pl.semaphore_signal(barrier, inc=1, device_id=(half + 1 + 2 * k, e, r), device_id_type=MESH)

    for c in own_w:
        c.start()
    first_in = pltpu.make_async_copy(ft_ref, inc, lsem.at[4])
    loss_in = pltpu.make_async_copy(lc_ref, cot, lsem.at[5])

    @pl.when(s == 0)
    def _():
        first_in.start()

    @pl.when(s == last)
    def _():
        loss_in.start()

    one, none = jnp.int32(1), jnp.int32(0)
    pl.semaphore_wait(
        barrier,
        3
        + jnp.where(inner, one, none)
        + jnp.where(from_next, one, none)
        + jnp.where(from_before, one, none)
        + jnp.where(up_relay, 2, 0)
        + jnp.where(down_relay, one, none)
        + jnp.where(s == half, relays, 0),
    )

    @pl.when(up_relay)
    def _():
        pl.semaphore_signal(ready, inc=1, device_id=(half - 1, e, r), device_id_type=MESH)

    hop_cot = remote(sc_ref, cot, ssem.at[0], srsem.at[0], (jnp.maximum(s - 1, 0), e, r))
    hop_inc = remote(so_ref, inc, ssem.at[1], srsem.at[1], (jnp.minimum(s + 1, last), e, r))

    @pl.when(from_before)
    def _():
        hop_cot.start()

    @pl.when(from_next)
    def _():
        hop_inc.start()

    step = TOK // relays

    def out_by(ref, k, section):
        return remote(ref.at[pl.ds(k * step, step)], relay, csend.at[k], rsem.at[0], (section, e, r))

    @pl.when(s == half)
    def _():
        for k in range(relays):
            out_by(sc_ref, k, 2 * k).start()

    def out_up():
        @pl.when(s == half - 1)
        def _():
            pl.semaphore_wait(ready, relays)
            for k in range(relays):
                out_by(so_ref, k, half + 1 + 2 * k).start()

    def in_by(dst, k, section):
        first = k * step if isinstance(k, int) else pl.multiple_of(k * step, step)
        return remote(relay, dst.at[pl.ds(first, step)], rsem.at[1], crecv.at[k], (section, e, r))

    def pass_relay():
        @pl.when(up_relay)
        def _():
            c = in_by(inc, relay_at, half)
            out_by(so_ref, 0, half).wait_recv()
            c.start()

        @pl.when(down_relay)
        def _():
            c = in_by(cot, relay_at, half - 1)
            out_by(sc_ref, 0, half).wait_recv()
            c.start()

    right, left = (s, e, xs[1]), (s, e, xs[3])
    up_half, low_half = pl.ds(0, HID // 2), pl.ds(HID // 2, HID // 2)
    w_refs = (gw_ref, uw_ref, dw_ref)

    def w_right(a, slot):
        return remote(w_refs[a], w.at[a, slot], wsend.at[a, 0], wrecv.at[a, 0], right)

    def w_left(a, slot):
        return remote(w_refs[a], w.at[a, slot], wsend.at[a, 1], wrecv.at[a, 1], left)

    def w_right_on(a, slot):
        ref = w.at[a, slot, up_half]
        return remote(ref, ref, wsend.at[a, 2], wrecv.at[a, 2], right)

    def w_left_on(a, slot):
        ref = w.at[a, slot, low_half]
        return remote(ref, ref, wsend.at[a, 3], wrecv.at[a, 3], left)

    for a in range(3):
        w_right(a, r).start()
        w_left(a, r).start()

    def w_pass(a):
        w_right(a, xs[3]).wait_recv()
        w_right_on(a, xs[3]).start()
        w_left(a, xs[1]).wait_recv()
        w_left_on(a, xs[1]).start()

    def w_arrived(a):
        own_w[a].wait()
        w_right_on(a, xs[2]).wait_recv()
        w_left_on(a, xs[2]).wait_recv()

    def w_sent(a):
        for make in (w_right, w_left, w_right_on, w_left_on):
            make(a, r).wait_send()

    ca = CAP // CA

    def z_copy(a, block, k, dev, c):
        ref = rows.at[a, block, pl.ds(c * ca, ca)]
        return remote(ref, ref, zsend.at[a, k, c], zrecv.at[a, block, c], (s, dev, r))

    def z_send(a, k, dev):
        for c in range(CA):
            z_copy(a, e, k, dev, c).start()

    def z_own(a):
        @pl.when(inner)
        def _():
            for c in range(CA):
                z_copy(a, e, 0, other, c).start()
                z_copy(a, e, 1, end, c).start()

        @pl.when(outer)
        def _():
            z_send(a, 0, near)

    def z_pass(a, *moves):
        @pl.when(inner)
        def _():
            for c in range(CA):
                for block, k, dev in moves:
                    copy = z_copy(a, block, k, dev, c)
                    copy.wait_recv()
                    copy.start()

    def normed_rows(pick, tokens):
        x = dot_nn(pick, tokens)
        return (x * inverse_rms(x) * gain_ref[...]).astype(BF)

    smalls[0].wait()
    smalls[1].wait()
    pick_b, pick_scale = slots(be_ref[...], bs_ref[...])
    load_kept.wait()
    smalls[2].wait()
    rows[0, e] = normed_rows(pick_b, kept[...])
    z_own(0)
    out_up()
    smalls[3].wait()
    smalls[4].wait()
    pick_f, _ = slots(fe_ref[...], fs_ref[...])
    z_pass(0, (end, 2, other), (other, 3, end))
    w_pass(0)

    late = s == half - 1
    punctual = jnp.logical_not(late)

    @pl.when(late)
    def _():
        w_pass(1)
        z_pass(0, (far, 4, end))
        hop_inc.wait_recv()
        rows[2, e] = normed_rows(pick_f, inc[...])
        z_own(2)

    @pl.when(s == last)
    def _():
        loss_in.wait()

    @pl.when(s == half - 1)
    def _():
        for k in range(relays):
            in_by(cot, k, half - 1).wait_recv()

    @pl.when(from_next)
    def _():
        hop_cot.wait_recv()

    rows[1, e] = (pick_scale * dot_nn(pick_b, cot[...])).astype(BF)
    z_own(1)

    @pl.when(punctual)
    def _():
        w_pass(1)
        z_pass(0, (far, 4, end))

    pass_relay()

    @pl.when(s == 0)
    def _():
        first_in.wait()

    @pl.when(s == half)
    def _():
        for k in range(relays):
            in_by(inc, k, half).wait_recv()

    @pl.when(from_before & punctual)
    def _():
        hop_inc.wait_recv()

    @pl.when(punctual)
    def _():
        rows[2, e] = normed_rows(pick_f, inc[...])

    @pl.when(outer & punctual)
    def _():
        z_send(2, 0, near)

    z_pass(1, (end, 2, other), (other, 3, end))
    w_pass(2)
    z_pass(2, (end, 2, other))

    @pl.when(inner & punctual)
    def _():
        z_send(2, 0, other)

    z_pass(1, (far, 4, end))

    def z_arrived(a, block):
        for c in range(CA):
            z_copy(a, block, 0, near, c).wait_recv()

    def project(a, group):
        total = None
        for k in range(4):
            prod = dot_nt(group[:, k * DS : (k + 1) * DS], w[a, k])
            total = prod if total is None else total + prod
        return total

    def backward_acts(group_in, group_grad):
        gate_act = project(0, group_in)
        up_act = project(1, group_in)
        squash = sigmoid(gate_act)
        act = gate_act * squash
        grad_hidden = project(2, group_grad)
        return (
            (grad_hidden * up_act * squash * (1.0 + gate_act * (1.0 - squash))).astype(BF),
            (grad_hidden * act).astype(BF),
            (act * up_act).astype(BF),
        )

    def forward_acts(group):
        g = project(0, group)
        return (g * sigmoid(g) * project(1, group)).astype(BF)

    def backward_part(grad_gate, grad_up, k):
        return (dot_nn(grad_gate, w[0, k]) + dot_nn(grad_up, w[1, k])).astype(BF)

    def forward_part(hidden, k):
        return dot_nn(hidden, w[2, k]).astype(BF)

    def backward_block(block):
        made = backward_acts(rows[0, block], rows[1, block])
        for a in range(3):
            acts[a, block] = made[a]
        for k in range(4):
            part[0, block, :, k * DS : (k + 1) * DS] = backward_part(made[0], made[1], k)

    def forward_block(block):
        hidden = forward_acts(rows[2, block])
        for k in range(4):
            part[1, block, :, k * DS : (k + 1) * DS] = forward_part(hidden, k)

    cr = CAP // CR

    def leg(j, src, dst, k, m, dev, c):
        return remote(src, dst.at[pl.ds(c * cr, cr)], psend.at[j, k, c], precv.at[j, m, c], (s, dev, r))

    def for_far(j, c):
        return leg(j, part.at[j, 3 - e, pl.ds(c * cr, cr)], mid.at[j, 0], 0, 0, near, c)

    def for_across(j, c):
        return leg(j, part.at[j, 3 - near, pl.ds(c * cr, cr)], mid.at[j, 1], 1, 1, near, c)

    def for_near(j, c):
        return leg(j, part.at[j, near, pl.ds(c * cr, cr)], got.at[j, 1], 2, 2, near, c)

    def on_far(j, c):
        return leg(j, part.at[j, far, pl.ds(c * cr, cr)], mid.at[j, 2], 0, 3, other, c)

    def on_other(j, c):
        return leg(j, part.at[j, other, pl.ds(c * cr, cr)], got.at[j, 2], 1, 4, other, c)

    def on_end(j, c):
        return leg(j, part.at[j, end, pl.ds(c * cr, cr)], got.at[j, 1], 2, 2, end, c)

    def add_mid(j, dest, m, c):
        here = pl.ds(c * cr, cr)
        part[j, dest, here, :] = (part[j, dest, here, :].astype(F32) + mid[j, m, here, :].astype(F32)).astype(BF)

    def pass_term(j, dest, m, arriving, leaving):
        for c in range(CR):
            arriving(j, c).wait_recv()
            add_mid(j, dest, m, c)
            leaving(j, c).start()

    def send_term(j, make):
        for c in range(CR):
            make(j, c).start()

    def parts_arrived(j):
        for c in range(CR):
            for_near(j, c).wait_recv()

        @pl.when(inner)
        def _():
            for c in range(CR):
                on_other(j, c).wait_recv()

    def parts_sent(j):
        for k in range(3):
            for c in range(CR):
                leg(j, part.at[j, 0, pl.ds(c * cr, cr)], mid.at[j, 0], k, 0, near, c).wait_send()

    def d_far(a, h):
        half_rows = (up_half, low_half)[h]
        return remote(
            dwst.at[a, xs[2], half_rows], dwmid.at[a, h], dsend.at[a, h], drecv.at[a, h], (right, left)[h]
        )

    def d_near(a, h, joined):
        half_rows = (up_half, low_half)[h if joined else 1 - h]
        n = 2 + 2 * h + (1 if joined else 0)
        return remote(
            dwst.at[a, (xs[1], xs[3])[h], half_rows],
            dwgot.at[a, h, half_rows],
            dsend.at[a, n],
            drecv.at[a, n],
            (right, left)[h],
        )

    def send_weight_grads():
        group_in, group_grad = rows[0].reshape(4 * CAP, D), rows[1].reshape(4 * CAP, D)
        for a, group in enumerate((group_in, group_in, group_grad)):
            act = acts[a].reshape(4 * CAP, HID)
            for k in range(4):
                dwst[a, k] = dot_tt(act, group[:, k * DS : (k + 1) * DS]).astype(BF)
            for h in range(2):
                d_far(a, h).start()

    def send_weight_grads_near():
        for a in range(3):
            for h in range(2):
                d_near(a, h, False).start()

    def join_weight_grads():
        for a in range(3):
            for h in range(2):
                d_far(a, h).wait_recv()
                half_rows, to = (up_half, low_half)[h], (xs[1], xs[3])[h]
                joined = dwst[a, to, half_rows, :].astype(F32) + dwmid[a, h].astype(F32)
                dwst[a, to, half_rows, :] = joined.astype(BF)
                d_near(a, h, True).start()

    gain = gain_ref[...]
    table_b, scale_b = tables(be_ref[...], bs_ref[...])
    table_f, scale_f = tables(fe_ref[...], fs_ref[...])
    rscale_b = inverse_rms(kept[...].astype(F32))

    for a in range(3):
        w_arrived(a)

    @pl.when(outer)
    def _():
        got[0, 2] = jnp.zeros((CAP, D), BF)
        got[1, 2] = jnp.zeros((CAP, D), BF)
        for block, make in ((near, for_near), (3 - near, for_across), (3 - e, for_far)):
            z_arrived(0, block)
            z_arrived(1, block)
            backward_block(block)
            send_term(0, make)
        backward_block(e)
        send_weight_grads()
        for block, make in ((3 - e, for_far), (3 - near, for_across), (near, for_near)):
            z_arrived(2, block)
            forward_block(block)
            send_term(1, make)
            if make is for_far:
                send_weight_grads_near()
            if make is for_across:
                join_weight_grads()
        forward_block(e)

    @pl.when(inner)
    def _():
        made = backward_acts(rows[0].reshape(4 * CAP, D), rows[1].reshape(4 * CAP, D))
        for a in range(3):
            acts[a] = made[a].reshape(4, CAP, HID)
        for k in range(4):
            part[0, :, :, k * DS : (k + 1) * DS] = backward_part(made[0], made[1], k).reshape(4, CAP, DS)
        send_weight_grads()

    z_pass(2, (far, 4, end))
    z_pass(2, (other, 3, end))

    @pl.when(inner & punctual)
    def _():
        z_send(2, 1, end)

    @pl.when(inner)
    def _():
        hidden = forward_acts(rows[2].reshape(4 * CAP, D))
        for k in range(4):
            part[1, :, :, k * DS : (k + 1) * DS] = forward_part(hidden, k).reshape(4, CAP, DS)
        send_weight_grads_near()
        pass_term(0, other, 1, for_across, on_other)
        join_weight_grads()
        pass_term(0, far, 0, for_far, on_far)
        pass_term(0, end, 2, on_far, on_end)
        pass_term(1, far, 0, for_far, on_far)

    got[0, 0] = part[0, e]
    got[1, 0] = part[1, e]

    parts_arrived(0)
    grad_normed = dot_nn(table_b[:, : 3 * CAP], got[0].reshape(3 * CAP, D))
    xhat = kept[...].astype(F32) * rscale_b
    gst[0, 0] = jnp.sum(grad_normed * xhat, axis=0, keepdims=True)
    gain_z = []
    for d in (1, 2, 3):
        c = remote(gst.at[0, 0], gst.at[0, d], gsend.at[0, d], grecv.at[0, d], (s, zs[d], r))
        c.start()
        gain_z.append(c)
    gx = grad_normed * gain
    mean = jnp.mean(gx * xhat, axis=1, keepdims=True)
    ig[...] = (cot[...].astype(F32) + rscale_b * (gx - xhat * mean)).astype(BF)
    out_ig = pltpu.make_async_copy(ig, ig_ref, osem.at[0])
    out_ig.start()

    @pl.when(inner)
    def _():
        pass_term(1, other, 1, for_across, on_other)
        pass_term(1, end, 2, on_far, on_end)

    for c in gain_z:
        c.wait_recv()
    gst[1, 0] = (gst[0, 0] + gst[0, 1]) + (gst[0, 2] + gst[0, 3])
    gain_x = []
    for d in (1, 2, 3):
        c = remote(gst.at[1, 0], gst.at[1, d], gsend.at[1, d], grecv.at[1, d], (s, e, xs[d]))
        c.start()
        gain_x.append(c)

    parts_arrived(1)
    tokens = dot_nn(table_f[:, : 3 * CAP], got[1].reshape(3 * CAP, D))
    lo[...] = (inc[...].astype(F32) + scale_f * tokens).astype(BF)
    out_lo = pltpu.make_async_copy(lo, lo_ref, osem.at[1])
    out_lo.start()
    outs = [out_ig, out_lo]

    for a, ref in enumerate((gg_ref, ug_ref, dg_ref)):
        for h in range(2):
            d_near(a, h, False).wait_recv()
            d_near(a, h, True).wait_recv()
        total = dwst[a, r].astype(F32) + (dwgot[a, 0].astype(F32) + dwgot[a, 1].astype(F32))
        dwout[a] = total.astype(BF)
        c = pltpu.make_async_copy(dwout.at[a], ref, osem.at[2 + a])
        c.start()
        outs.append(c)
    for c in gain_x:
        c.wait_recv()
    gout[...] = (gst[1, 0] + gst[1, 1]) + (gst[1, 2] + gst[1, 3])
    c = pltpu.make_async_copy(gout, gt_ref, osem.at[5])
    c.start()
    outs.append(c)

    @pl.when(from_before)
    def _():
        hop_cot.wait_send()

    @pl.when(from_next)
    def _():
        hop_inc.wait_send()

    @pl.when((s == half) | (s == half - 1))
    def _():
        for k in range(relays):
            out_by(so_ref, k, half).wait_send()

    @pl.when(up_relay | down_relay)
    def _():
        in_by(inc, 0, half).wait_send()

    parts_sent(0)
    parts_sent(1)

    for a in range(3):
        w_sent(a)
        for h in range(2):
            d_far(a, h).wait_send()
            d_near(a, h, False).wait_send()
            d_near(a, h, True).wait_send()
    for c in gain_z + gain_x:
        c.wait_send()
    for a in range(3):
        for c in range(CA):
            z_copy(a, e, 0, near, c).wait_send()

        @pl.when(inner)
        def _():
            for k in range(1, 5):
                for c in range(CA):
                    z_copy(a, e, k, end, c).wait_send()

    for c in outs:
        c.wait()


def finish(*refs):
    ins, outs, held, sems = refs[:6], refs[6:12], refs[12:18], refs[18]
    loads = [pltpu.make_async_copy(ins[i], held[i], sems.at[0, i]) for i in range(6)]
    stores = [pltpu.make_async_copy(held[i], outs[i], sems.at[1, i]) for i in range(6)]
    for c in loads:
        c.start()
    for load, store in zip(loads, stores):
        load.wait()
        store.start()
    for c in stores:
        c.wait()


def local(so, ft, kept, sc, lc, gain, gw, uw, dw, fe, fs, be, bs):
    any_spec = pl.BlockSpec(memory_space=pl.ANY)
    dma = pltpu.SemaphoreType.DMA
    outs = pl.pallas_call(
        kernel,
        out_shape=(
            jax.ShapeDtypeStruct((TOK, D), BF),
            jax.ShapeDtypeStruct((TOK, D), BF),
            jax.ShapeDtypeStruct((HID, DS), BF),
            jax.ShapeDtypeStruct((HID, DS), BF),
            jax.ShapeDtypeStruct((HID, DS), BF),
            jax.ShapeDtypeStruct((1, D), F32),
        ),
        in_specs=[any_spec] * 13,
        out_specs=[any_spec] * 6,
        scratch_shapes=[
            pltpu.VMEM((TOP, TOK), jnp.int32),
            pltpu.VMEM((TOP, TOK), F32),
            pltpu.VMEM((TOP, TOK), jnp.int32),
            pltpu.VMEM((TOP, TOK), F32),
            pltpu.VMEM((1, D), F32),
            pltpu.VMEM((TOK, D), BF),
            pltpu.VMEM((TOK, D), BF),
            pltpu.VMEM((TOK, D), BF),
            pltpu.VMEM((3, 4, HID, DS), BF),
            pltpu.VMEM((3, 4, CAP, D), BF),
            pltpu.VMEM((2, 4, CAP, D), BF),
            pltpu.VMEM((2, 3, CAP, D), BF),
            pltpu.VMEM((2, 3, CAP, D), BF),
            pltpu.VMEM((16, D), BF),
            pltpu.VMEM((3, 4, CAP, HID), BF),
            pltpu.VMEM((3, 4, HID, DS), BF),
            pltpu.VMEM((3, 2, HID // 2, DS), BF),
            pltpu.VMEM((3, 2, HID, DS), BF),
            pltpu.VMEM((3, HID, DS), BF),
            pltpu.VMEM((TOK, D), BF),
            pltpu.VMEM((TOK, D), BF),
            pltpu.VMEM((2, 4, 1, D), F32),
            pltpu.VMEM((1, D), F32),
            dma((11,)),
            dma((6,)),
            dma((2,)),
            dma((2,)),
            dma((3, 4)),
            dma((3, 4)),
            dma((3, 5, CA)),
            dma((3, 4, CA)),
            dma((2, 3, CR)),
            dma((2, 5, CR)),
            dma((8,)),
            dma((8,)),
            dma((2,)),
            pltpu.SemaphoreType.REGULAR,
            dma((3, 6)),
            dma((3, 6)),
            dma((2, 4)),
            dma((2, 4)),
        ],
        compiler_params=pltpu.CompilerParams(
            collective_id=0, has_side_effects=True, vmem_limit_bytes=60 << 20
        ),
        name="relay",
    )(
        so.reshape(TOK, D), ft.reshape(TOK, D), kept.reshape(TOK, D), sc.reshape(TOK, D), lc.reshape(TOK, D),
        gain.reshape(1, D), gw[0], uw[0], dw[0], fe[0, 0].T, fs[0, 0].T, be[0, 0].T, bs[0, 0].T,
    )
    outs = pl.pallas_call(
        finish,
        out_shape=tuple(jax.ShapeDtypeStruct(o.shape, o.dtype) for o in outs),
        in_specs=[any_spec] * 6,
        out_specs=[any_spec] * 6,
        scratch_shapes=[pltpu.VMEM(o.shape, o.dtype) for o in outs] + [dma((2, 6))],
        compiler_params=pltpu.CompilerParams(vmem_limit_bytes=60 << 20),
        name="finish",
    )(*outs)
    return (
        outs[0][None, None], outs[1][None, None], outs[2][None], outs[3][None], outs[4][None], outs[5],
    )


def solution(mesh):
    tokens = P("section", "dp", "expert", None)
    stored = P("section", "expert", "dp")
    first = P("dp", "expert", None)
    return jax.shard_map(
        local,
        mesh=mesh,
        in_specs=(tokens, first, tokens, tokens, first, P("section", None)) + (stored,) * 3 + (tokens,) * 4,
        out_specs=(tokens, tokens, stored, stored, stored, P("section", None)),
        check_vma=False,
    )
```

```python
import jax
import jax.numpy as jnp
from jax import lax
from jax.experimental import pallas as pl
from jax.experimental.pallas import tpu as pltpu
from jax.sharding import PartitionSpec as P

CAP = 48
TOP = 8
TOK = 128
D = 2048
HID = 192
DS = 512
EPS = 1e-06
CA = 3
CR = 3
MESH = pl.DeviceIdType.MESH
BF = jnp.bfloat16
F32 = jnp.float32


def dot_tt(a, b):
    return lax.dot_general(a, b, (((0,), (0,)), ((), ())), preferred_element_type=F32)


def dot_nt(a, b):
    return lax.dot_general(a, b, (((1,), (1,)), ((), ())), preferred_element_type=F32)


def dot_nn(a, b):
    return jnp.dot(a, b, preferred_element_type=F32)


def tables(chosen, weights):
    chosen, weights = chosen.T, weights.T
    picked = chosen == 0
    routed = jnp.max(picked.astype(F32), axis=1, keepdims=True)
    scale = jnp.sum(jnp.where(picked, weights, 0.0), axis=1, keepdims=True)
    row = lax.broadcasted_iota(jnp.int32, (TOK, TOK), 0)
    col = lax.broadcasted_iota(jnp.int32, (TOK, TOK), 1)
    lower = (col <= row).astype(BF)
    count = dot_nn(lower, jnp.broadcast_to(routed, (TOK, TOK)).astype(BF))[:, :1]
    slot = jnp.where(routed > 0.5, count - 1.0, -1.0)
    place = lax.broadcasted_iota(jnp.int32, (TOK, 4 * CAP), 1)
    place = (
        place
        - CAP * (place >= CAP).astype(jnp.int32)
        - CAP * (place >= 2 * CAP).astype(jnp.int32)
        - CAP * (place >= 3 * CAP).astype(jnp.int32)
    )
    table = jnp.where(slot == place.astype(F32), 1.0, 0.0).astype(BF)
    return table, scale


def slots(chosen, weights):
    picked = chosen == 0
    routed = jnp.max(picked.astype(F32), axis=0, keepdims=True)
    scale = jnp.sum(jnp.where(picked, weights, 0.0), axis=0, keepdims=True)
    row = lax.broadcasted_iota(jnp.int32, (TOK, TOK), 0)
    col = lax.broadcasted_iota(jnp.int32, (TOK, TOK), 1)
    upper = (row <= col).astype(BF)
    count = dot_nn(jnp.broadcast_to(routed, (TOP, TOK)).astype(BF), upper)[:1]
    slot = jnp.where(routed > 0.5, count - 1.0, -1.0)
    hit = slot == lax.broadcasted_iota(jnp.int32, (CAP, TOK), 0).astype(F32)
    return jnp.where(hit, 1.0, 0.0).astype(BF), jnp.sum(jnp.where(hit, scale, 0.0), axis=1, keepdims=True)


def inverse_rms(x):
    return lax.rsqrt(jnp.mean(x * x, axis=1, keepdims=True) + EPS)


def sigmoid(v):
    return 1.0 / (1.0 + jnp.exp(-v))


def kernel(
    so_ref, ft_ref, kept_ref, sc_ref, lc_ref, gain_in, gw_ref, uw_ref, dw_ref, fe_in, fs_in, be_in, bs_in,
    lo_ref, ig_ref, gg_ref, ug_ref, dg_ref, gt_ref,
    fe_ref, fs_ref, be_ref, bs_ref, gain_ref, kept, cot, inc, w, rows, part, got, mid, relay, acts, dwst, dwmid, dwgot, dwout, lo, ig, gst, gout,
    lsem, osem, ssem, srsem, wsend, wrecv, zsend, zrecv, psend, precv, csend, crecv, rsem, ready, dsend, drecv, gsend, grecv,
):
    s, e, r = lax.axis_index("section"), lax.axis_index("expert"), lax.axis_index("dp")
    last = lax.axis_size("section") - 1
    inner = (e == 1) | (e == 2)
    outer = jnp.logical_not(inner)
    end = jnp.where(e == 1, 0, 3)
    other = 3 - e
    far = 3 - end
    near = jnp.where(e == 0, 1, 2)

    def remote(src, dst, ss, rs, dev):
        return pltpu.make_async_remote_copy(
            src_ref=src, dst_ref=dst, send_sem=ss, recv_sem=rs, device_id=dev, device_id_type=MESH
        )

    xs = [lax.rem(r + d, 4) for d in range(4)]
    zs = [lax.rem(e + d, 4) for d in range(4)]

    own_w = [pltpu.make_async_copy(ref, w.at[a, r], lsem.at[1 + a]) for a, ref in enumerate((gw_ref, uw_ref, dw_ref))]
    load_kept = pltpu.make_async_copy(kept_ref, kept, lsem.at[0])
    smalls = [
        pltpu.make_async_copy(src, dst, lsem.at[6 + i])
        for i, (src, dst) in enumerate(
            ((be_in, be_ref), (bs_in, bs_ref), (gain_in, gain_ref), (fe_in, fe_ref), (fs_in, fs_ref))
        )
    ]
    smalls[0].start()
    smalls[1].start()
    load_kept.start()
    for c in smalls[2:]:
        c.start()
    barrier = pltpu.get_barrier_semaphore()
    for d in (1, 3):
        pl.semaphore_signal(barrier, inc=1, device_id=(s, e, xs[d]), device_id_type=MESH)

    @pl.when(outer)
    def _():
        pl.semaphore_signal(barrier, inc=1, device_id=(s, near, r), device_id_type=MESH)

    @pl.when(inner)
    def _():
        pl.semaphore_signal(barrier, inc=1, device_id=(s, other, r), device_id_type=MESH)
        pl.semaphore_signal(barrier, inc=1, device_id=(s, end, r), device_id_type=MESH)

    from_next = (s < last) & (s != last // 2)
    from_before = (s > 0) & (s != last // 2 + 1)

    @pl.when(from_next)
    def _():
        pl.semaphore_signal(barrier, inc=1, device_id=(s + 1, e, r), device_id_type=MESH)

    @pl.when(from_before)
    def _():
        pl.semaphore_signal(barrier, inc=1, device_id=(s - 1, e, r), device_id_type=MESH)

    half = (last + 1) // 2
    relays = half // 2
    up_relay = (s > half) & (lax.rem(s, 2) == 1)
    down_relay = (s < half) & (lax.rem(s, 2) == 0)
    relay_at = jnp.where(s > half, s - half, s) // 2

    @pl.when(down_relay)
    def _():
        pl.semaphore_signal(barrier, inc=1, device_id=(half, e, r), device_id_type=MESH)

    @pl.when(s == half)
    def _():
        for k in range(relays):
            pl.semaphore_signal(barrier, inc=1, device_id=(half + 1 + 2 * k, e, r), device_id_type=MESH)

    @pl.when(s == half - 1)
    def _():
        for k in range(relays):
            pl.semaphore_signal(barrier, inc=1, device_id=(2 * k, e, r), device_id_type=MESH)
            pl.semaphore_signal(barrier, inc=1, device_id=(half + 1 + 2 * k, e, r), device_id_type=MESH)

    for c in own_w:
        c.start()
    first_in = pltpu.make_async_copy(ft_ref, inc, lsem.at[4])
    loss_in = pltpu.make_async_copy(lc_ref, cot, lsem.at[5])

    @pl.when(s == 0)
    def _():
        first_in.start()

    @pl.when(s == last)
    def _():
        loss_in.start()

    one, none = jnp.int32(1), jnp.int32(0)
    pl.semaphore_wait(
        barrier,
        3
        + jnp.where(inner, one, none)
        + jnp.where(from_next, one, none)
        + jnp.where(from_before, one, none)
        + jnp.where(up_relay, 2, 0)
        + jnp.where(down_relay, one, none)
        + jnp.where(s == half, relays, 0),
    )

    @pl.when(up_relay)
    def _():
        pl.semaphore_signal(ready, inc=1, device_id=(half - 1, e, r), device_id_type=MESH)

    hop_cot = remote(sc_ref, cot, ssem.at[0], srsem.at[0], (jnp.maximum(s - 1, 0), e, r))
    hop_inc = remote(so_ref, inc, ssem.at[1], srsem.at[1], (jnp.minimum(s + 1, last), e, r))

    @pl.when(from_before)
    def _():
        hop_cot.start()

    @pl.when(from_next)
    def _():
        hop_inc.start()

    step = TOK // relays

    def out_by(ref, k, section):
        return remote(ref.at[pl.ds(k * step, step)], relay, csend.at[k], rsem.at[0], (section, e, r))

    @pl.when(s == half)
    def _():
        for k in range(relays):
            out_by(sc_ref, k, 2 * k).start()

    def out_up():
        pl.semaphore_wait(ready, relays)
        for k in range(relays):
            out_by(so_ref, k, half + 1 + 2 * k).start()

    def in_by(dst, k, section):
        first = k * step if isinstance(k, int) else pl.multiple_of(k * step, step)
        return remote(relay, dst.at[pl.ds(first, step)], rsem.at[1], crecv.at[k], (section, e, r))

    def pass_relay():
        @pl.when(up_relay)
        def _():
            c = in_by(inc, relay_at, half)
            out_by(so_ref, 0, half).wait_recv()
            c.start()

        @pl.when(down_relay)
        def _():
            c = in_by(cot, relay_at, half - 1)
            out_by(sc_ref, 0, half).wait_recv()
            c.start()

    right, left = (s, e, xs[1]), (s, e, xs[3])
    up_half, low_half = pl.ds(0, HID // 2), pl.ds(HID // 2, HID // 2)
    w_refs = (gw_ref, uw_ref, dw_ref)

    def w_right(a, slot):
        return remote(w_refs[a], w.at[a, slot], wsend.at[a, 0], wrecv.at[a, 0], right)

    def w_left(a, slot):
        return remote(w_refs[a], w.at[a, slot], wsend.at[a, 1], wrecv.at[a, 1], left)

    def w_right_on(a, slot):
        ref = w.at[a, slot, up_half]
        return remote(ref, ref, wsend.at[a, 2], wrecv.at[a, 2], right)

    def w_left_on(a, slot):
        ref = w.at[a, slot, low_half]
        return remote(ref, ref, wsend.at[a, 3], wrecv.at[a, 3], left)

    for a in range(3):
        w_right(a, r).start()
        w_left(a, r).start()

    def w_pass(a):
        w_right(a, xs[3]).wait_recv()
        w_right_on(a, xs[3]).start()
        w_left(a, xs[1]).wait_recv()
        w_left_on(a, xs[1]).start()

    def w_arrived(a):
        own_w[a].wait()
        w_right_on(a, xs[2]).wait_recv()
        w_left_on(a, xs[2]).wait_recv()

    def w_sent(a):
        for make in (w_right, w_left, w_right_on, w_left_on):
            make(a, r).wait_send()

    ca = CAP // CA

    def z_copy(a, block, k, dev, c):
        ref = rows.at[a, block, pl.ds(c * ca, ca)]
        return remote(ref, ref, zsend.at[a, k, c], zrecv.at[a, block, c], (s, dev, r))

    def z_send(a, k, dev):
        for c in range(CA):
            z_copy(a, e, k, dev, c).start()

    def z_own(a):
        @pl.when(inner)
        def _():
            for c in range(CA):
                z_copy(a, e, 0, other, c).start()
                z_copy(a, e, 1, end, c).start()

        @pl.when(outer)
        def _():
            z_send(a, 0, near)

    def z_pass(a, *moves):
        @pl.when(inner)
        def _():
            for c in range(CA):
                for block, k, dev in moves:
                    copy = z_copy(a, block, k, dev, c)
                    copy.wait_recv()
                    copy.start()

    def normed_rows(pick, tokens):
        x = dot_nn(pick, tokens)
        return (x * inverse_rms(x) * gain_ref[...]).astype(BF)

    smalls[0].wait()
    smalls[1].wait()
    pick_b, pick_scale = slots(be_ref[...], bs_ref[...])
    load_kept.wait()
    smalls[2].wait()
    rows[0, e] = normed_rows(pick_b, kept[...])
    z_own(0)
    smalls[3].wait()
    smalls[4].wait()
    pick_f, _ = slots(fe_ref[...], fs_ref[...])
    z_pass(0, (end, 2, other), (other, 3, end))
    w_pass(0)

    late = s == half - 1
    punctual = jnp.logical_not(late)

    @pl.when(late)
    def _():
        w_pass(1)
        z_pass(0, (far, 4, end))
        hop_inc.wait_recv()
        rows[2, e] = normed_rows(pick_f, inc[...])
        z_own(2)
        out_up()

    @pl.when(s == last)
    def _():
        loss_in.wait()

    @pl.when(s == half - 1)
    def _():
        for k in range(relays):
            in_by(cot, k, half - 1).wait_recv()

    @pl.when(from_next)
    def _():
        hop_cot.wait_recv()

    rows[1, e] = (pick_scale * dot_nn(pick_b, cot[...])).astype(BF)
    z_own(1)

    @pl.when(punctual)
    def _():
        w_pass(1)
        z_pass(0, (far, 4, end))

    pass_relay()

    @pl.when(s == 0)
    def _():
        first_in.wait()

    @pl.when(from_before & punctual)
    def _():
        hop_inc.wait_recv()

    @pl.when(punctual & (s != half))
    def _():
        rows[2, e] = normed_rows(pick_f, inc[...])

    @pl.when(outer & punctual & (s != half))
    def _():
        z_send(2, 0, near)

    z_pass(1, (end, 2, other), (other, 3, end))
    w_pass(2)

    @pl.when(s != half)
    def _():
        z_pass(2, (end, 2, other))

    @pl.when(inner & punctual & (s != half))
    def _():
        z_send(2, 0, other)

    z_pass(1, (far, 4, end))

    @pl.when(s == half)
    def _():
        for k in range(relays):
            in_by(inc, k, half).wait_recv()
        rows[2, e] = normed_rows(pick_f, inc[...])

        @pl.when(outer)
        def _():
            z_send(2, 0, near)

        z_pass(2, (end, 2, other))

        @pl.when(inner)
        def _():
            z_send(2, 0, other)

    def z_arrived(a, block):
        for c in range(CA):
            z_copy(a, block, 0, near, c).wait_recv()

    def project(a, group):
        total = None
        for k in range(4):
            prod = dot_nt(group[:, k * DS : (k + 1) * DS], w[a, k])
            total = prod if total is None else total + prod
        return total

    def backward_acts(group_in, group_grad):
        gate_act = project(0, group_in)
        up_act = project(1, group_in)
        squash = sigmoid(gate_act)
        act = gate_act * squash
        grad_hidden = project(2, group_grad)
        return (
            (grad_hidden * up_act * squash * (1.0 + gate_act * (1.0 - squash))).astype(BF),
            (grad_hidden * act).astype(BF),
            (act * up_act).astype(BF),
        )

    def forward_acts(group):
        g = project(0, group)
        return (g * sigmoid(g) * project(1, group)).astype(BF)

    def backward_part(grad_gate, grad_up, k):
        return (dot_nn(grad_gate, w[0, k]) + dot_nn(grad_up, w[1, k])).astype(BF)

    def forward_part(hidden, k):
        return dot_nn(hidden, w[2, k]).astype(BF)

    def backward_block(block):
        made = backward_acts(rows[0, block], rows[1, block])
        for a in range(3):
            acts[a, block] = made[a]
        for k in range(4):
            part[0, block, :, k * DS : (k + 1) * DS] = backward_part(made[0], made[1], k)

    def forward_block(block):
        hidden = forward_acts(rows[2, block])
        for k in range(4):
            part[1, block, :, k * DS : (k + 1) * DS] = forward_part(hidden, k)

    cr = CAP // CR

    def leg(j, src, dst, k, m, dev, c):
        return remote(src, dst.at[pl.ds(c * cr, cr)], psend.at[j, k, c], precv.at[j, m, c], (s, dev, r))

    def for_far(j, c):
        return leg(j, part.at[j, 3 - e, pl.ds(c * cr, cr)], mid.at[j, 0], 0, 0, near, c)

    def for_across(j, c):
        return leg(j, part.at[j, 3 - near, pl.ds(c * cr, cr)], mid.at[j, 1], 1, 1, near, c)

    def for_near(j, c):
        return leg(j, part.at[j, near, pl.ds(c * cr, cr)], got.at[j, 1], 2, 2, near, c)

    def on_far(j, c):
        return leg(j, part.at[j, far, pl.ds(c * cr, cr)], mid.at[j, 2], 0, 3, other, c)

    def on_other(j, c):
        return leg(j, part.at[j, other, pl.ds(c * cr, cr)], got.at[j, 2], 1, 4, other, c)

    def on_end(j, c):
        return leg(j, part.at[j, end, pl.ds(c * cr, cr)], got.at[j, 1], 2, 2, end, c)

    def add_mid(j, dest, m, c):
        here = pl.ds(c * cr, cr)
        part[j, dest, here, :] = (part[j, dest, here, :].astype(F32) + mid[j, m, here, :].astype(F32)).astype(BF)

    def pass_term(j, dest, m, arriving, leaving):
        for c in range(CR):
            arriving(j, c).wait_recv()
            add_mid(j, dest, m, c)
            leaving(j, c).start()

    def send_term(j, make):
        for c in range(CR):
            make(j, c).start()

    def parts_arrived(j):
        for c in range(CR):
            for_near(j, c).wait_recv()

        @pl.when(inner)
        def _():
            for c in range(CR):
                on_other(j, c).wait_recv()

    def parts_sent(j):
        for k in range(3):
            for c in range(CR):
                leg(j, part.at[j, 0, pl.ds(c * cr, cr)], mid.at[j, 0], k, 0, near, c).wait_send()

    def d_far(a, h):
        half_rows = (up_half, low_half)[h]
        return remote(
            dwst.at[a, xs[2], half_rows], dwmid.at[a, h], dsend.at[a, h], drecv.at[a, h], (right, left)[h]
        )

    def d_near(a, h, joined):
        half_rows = (up_half, low_half)[h if joined else 1 - h]
        n = 2 + 2 * h + (1 if joined else 0)
        return remote(
            dwst.at[a, (xs[1], xs[3])[h], half_rows],
            dwgot.at[a, h, half_rows],
            dsend.at[a, n],
            drecv.at[a, n],
            (right, left)[h],
        )

    def send_weight_grads():
        group_in, group_grad = rows[0].reshape(4 * CAP, D), rows[1].reshape(4 * CAP, D)
        for a, group in enumerate((group_in, group_in, group_grad)):
            act = acts[a].reshape(4 * CAP, HID)
            for k in range(4):
                dwst[a, k] = dot_tt(act, group[:, k * DS : (k + 1) * DS]).astype(BF)
            for h in range(2):
                d_far(a, h).start()

    def send_weight_grads_near():
        for a in range(3):
            for h in range(2):
                d_near(a, h, False).start()

    def join_weight_grads():
        for a in range(3):
            for h in range(2):
                d_far(a, h).wait_recv()
                half_rows, to = (up_half, low_half)[h], (xs[1], xs[3])[h]
                joined = dwst[a, to, half_rows, :].astype(F32) + dwmid[a, h].astype(F32)
                dwst[a, to, half_rows, :] = joined.astype(BF)
                d_near(a, h, True).start()

    gain = gain_ref[...]
    table_b, scale_b = tables(be_ref[...], bs_ref[...])
    table_f, scale_f = tables(fe_ref[...], fs_ref[...])
    rscale_b = inverse_rms(kept[...].astype(F32))

    for a in range(3):
        w_arrived(a)

    gain_z = [remote(gst.at[0, 0], gst.at[0, d], gsend.at[0, d], grecv.at[0, d], (s, zs[d], r)) for d in (1, 2, 3)]
    gain_x = [remote(gst.at[1, 0], gst.at[1, d], gsend.at[1, d], grecv.at[1, d], (s, e, xs[d])) for d in (1, 2, 3)]

    def send_gain():
        terms = part[0].reshape(4 * CAP, D).astype(F32) * rows[0].reshape(4 * CAP, D).astype(F32)
        gst[0, 0] = jnp.sum(terms, axis=0, keepdims=True) / gain
        for c in gain_z:
            c.start()

    def pass_gain():
        for c in gain_z:
            c.wait_recv()
        gst[1, 0] = (gst[0, 0] + gst[0, 1]) + (gst[0, 2] + gst[0, 3])
        for c in gain_x:
            c.start()

    @pl.when(outer)
    def _():
        got[0, 2] = jnp.zeros((CAP, D), BF)
        got[1, 2] = jnp.zeros((CAP, D), BF)
        for block, make in ((near, for_near), (3 - near, for_across), (3 - e, for_far)):
            z_arrived(0, block)
            z_arrived(1, block)
            backward_block(block)
            send_term(0, make)
            if make is for_near:
                backward_block(e)
        send_weight_grads()
        send_gain()
        for block, make in ((3 - e, for_far), (3 - near, for_across), (near, for_near)):
            z_arrived(2, block)
            forward_block(block)
            send_term(1, make)
            if make is for_far:
                send_weight_grads_near()
                forward_block(e)
            if make is for_across:
                join_weight_grads()
                pass_gain()

    @pl.when(inner)
    def _():
        made = backward_acts(rows[0].reshape(4 * CAP, D), rows[1].reshape(4 * CAP, D))
        for a in range(3):
            acts[a] = made[a].reshape(4, CAP, HID)
        for k in range(4):
            part[0, :, :, k * DS : (k + 1) * DS] = backward_part(made[0], made[1], k).reshape(4, CAP, DS)
        send_weight_grads()
        send_gain()

    z_pass(2, (far, 4, end))
    z_pass(2, (other, 3, end))

    @pl.when(inner & punctual)
    def _():
        z_send(2, 1, end)

    @pl.when(inner)
    def _():
        hidden = forward_acts(rows[2].reshape(4 * CAP, D))
        for k in range(4):
            part[1, :, :, k * DS : (k + 1) * DS] = forward_part(hidden, k).reshape(4, CAP, DS)
        send_weight_grads_near()
        pass_term(0, other, 1, for_across, on_other)
        join_weight_grads()
        pass_term(0, far, 0, for_far, on_far)
        pass_gain()
        pass_term(0, end, 2, on_far, on_end)
        pass_term(1, far, 0, for_far, on_far)

    got[0, 0] = part[0, e]
    got[1, 0] = part[1, e]

    parts_arrived(0)
    grad_normed = dot_nn(table_b[:, : 3 * CAP], got[0].reshape(3 * CAP, D))
    xhat = kept[...].astype(F32) * rscale_b
    gx = grad_normed * gain
    mean = jnp.mean(gx * xhat, axis=1, keepdims=True)
    ig[...] = (cot[...].astype(F32) + rscale_b * (gx - xhat * mean)).astype(BF)
    out_ig = pltpu.make_async_copy(ig, ig_ref, osem.at[0])
    out_ig.start()

    @pl.when(inner)
    def _():
        pass_term(1, other, 1, for_across, on_other)
        pass_term(1, end, 2, on_far, on_end)

    parts_arrived(1)
    tokens = dot_nn(table_f[:, : 3 * CAP], got[1].reshape(3 * CAP, D))
    lo[...] = (inc[...].astype(F32) + scale_f * tokens).astype(BF)
    out_lo = pltpu.make_async_copy(lo, lo_ref, osem.at[1])
    out_lo.start()
    outs = [out_ig, out_lo]

    for a, ref in enumerate((gg_ref, ug_ref, dg_ref)):
        for h in range(2):
            d_near(a, h, False).wait_recv()
            d_near(a, h, True).wait_recv()
        total = dwst[a, r].astype(F32) + (dwgot[a, 0].astype(F32) + dwgot[a, 1].astype(F32))
        dwout[a] = total.astype(BF)
        c = pltpu.make_async_copy(dwout.at[a], ref, osem.at[2 + a])
        c.start()
        outs.append(c)
    for c in gain_x:
        c.wait_recv()
    gout[...] = (gst[1, 0] + gst[1, 1]) + (gst[1, 2] + gst[1, 3])
    c = pltpu.make_async_copy(gout, gt_ref, osem.at[5])
    c.start()
    outs.append(c)

    @pl.when(from_before)
    def _():
        hop_cot.wait_send()

    @pl.when(from_next)
    def _():
        hop_inc.wait_send()

    @pl.when((s == half) | (s == half - 1))
    def _():
        for k in range(relays):
            out_by(so_ref, k, half).wait_send()

    @pl.when(up_relay | down_relay)
    def _():
        in_by(inc, 0, half).wait_send()

    parts_sent(0)
    parts_sent(1)

    for a in range(3):
        w_sent(a)
        for h in range(2):
            d_far(a, h).wait_send()
            d_near(a, h, False).wait_send()
            d_near(a, h, True).wait_send()
    for c in gain_z + gain_x:
        c.wait_send()
    for a in range(3):
        for c in range(CA):
            z_copy(a, e, 0, near, c).wait_send()

        @pl.when(inner)
        def _():
            for k in range(1, 5):
                for c in range(CA):
                    z_copy(a, e, k, end, c).wait_send()

    for c in outs:
        c.wait()


def finish(*refs):
    copies = [pltpu.make_async_copy(refs[i], refs[6 + i], refs[12].at[i]) for i in range(6)]
    for c in copies:
        c.start()
    for c in copies:
        c.wait()


def local(so, ft, kept, sc, lc, gain, gw, uw, dw, fe, fs, be, bs):
    any_spec = pl.BlockSpec(memory_space=pl.ANY)
    dma = pltpu.SemaphoreType.DMA
    hbm = lambda x: pltpu.with_memory_space_constraint(x, pltpu.HBM)
    outs = pl.pallas_call(
        kernel,
        out_shape=(
            jax.ShapeDtypeStruct((TOK, D), BF),
            jax.ShapeDtypeStruct((TOK, D), BF),
            jax.ShapeDtypeStruct((HID, DS), BF),
            jax.ShapeDtypeStruct((HID, DS), BF),
            jax.ShapeDtypeStruct((HID, DS), BF),
            jax.ShapeDtypeStruct((1, D), F32),
        ),
        in_specs=[any_spec] * 13,
        out_specs=[any_spec] * 6,
        scratch_shapes=[
            pltpu.VMEM((TOP, TOK), jnp.int32),
            pltpu.VMEM((TOP, TOK), F32),
            pltpu.VMEM((TOP, TOK), jnp.int32),
            pltpu.VMEM((TOP, TOK), F32),
            pltpu.VMEM((1, D), F32),
            pltpu.VMEM((TOK, D), BF),
            pltpu.VMEM((TOK, D), BF),
            pltpu.VMEM((TOK, D), BF),
            pltpu.VMEM((3, 4, HID, DS), BF),
            pltpu.VMEM((3, 4, CAP, D), BF),
            pltpu.VMEM((2, 4, CAP, D), BF),
            pltpu.VMEM((2, 3, CAP, D), BF),
            pltpu.VMEM((2, 3, CAP, D), BF),
            pltpu.VMEM((16, D), BF),
            pltpu.VMEM((3, 4, CAP, HID), BF),
            pltpu.VMEM((3, 4, HID, DS), BF),
            pltpu.VMEM((3, 2, HID // 2, DS), BF),
            pltpu.VMEM((3, 2, HID, DS), BF),
            pltpu.VMEM((3, HID, DS), BF),
            pltpu.VMEM((TOK, D), BF),
            pltpu.VMEM((TOK, D), BF),
            pltpu.VMEM((2, 4, 1, D), F32),
            pltpu.VMEM((1, D), F32),
            dma((11,)),
            dma((6,)),
            dma((2,)),
            dma((2,)),
            dma((3, 4)),
            dma((3, 4)),
            dma((3, 5, CA)),
            dma((3, 4, CA)),
            dma((2, 3, CR)),
            dma((2, 5, CR)),
            dma((8,)),
            dma((8,)),
            dma((2,)),
            pltpu.SemaphoreType.REGULAR,
            dma((3, 6)),
            dma((3, 6)),
            dma((2, 4)),
            dma((2, 4)),
        ],
        compiler_params=pltpu.CompilerParams(
            collective_id=0, has_side_effects=True, vmem_limit_bytes=40 << 20
        ),
        name="relay",
    )(
        hbm(so.reshape(TOK, D)), hbm(ft.reshape(TOK, D)), hbm(kept.reshape(TOK, D)), hbm(sc.reshape(TOK, D)),
        hbm(lc.reshape(TOK, D)), hbm(gain.reshape(1, D)), hbm(gw[0]), hbm(uw[0]), hbm(dw[0]),
        hbm(fe[0, 0].T), hbm(fs[0, 0].T), hbm(be[0, 0].T), hbm(bs[0, 0].T),
    )
    outs = pl.pallas_call(
        finish,
        out_shape=tuple(jax.ShapeDtypeStruct(o.shape, o.dtype) for o in outs),
        in_specs=[any_spec] * 6,
        out_specs=[any_spec] * 6,
        scratch_shapes=[dma((6,))],
        compiler_params=pltpu.CompilerParams(vmem_limit_bytes=16 << 20),
        name="finish",
    )(*[pltpu.with_memory_space_constraint(o, pltpu.VMEM) for o in outs])
    return (
        outs[0][None, None], outs[1][None, None], outs[2][None], outs[3][None], outs[4][None], outs[5],
    )


def solution(mesh):
    tokens = P("section", "dp", "expert", None)
    stored = P("section", "expert", "dp")
    first = P("dp", "expert", None)
    return jax.shard_map(
        local,
        mesh=mesh,
        in_specs=(tokens, first, tokens, tokens, first, P("section", None)) + (stored,) * 3 + (tokens,) * 4,
        out_specs=(tokens, tokens, stored, stored, stored, P("section", None)),
        check_vma=False,
    )
```

```python
import jax
import jax.numpy as jnp
from jax import lax
from jax.experimental import pallas as pl
from jax.experimental.pallas import tpu as pltpu
from jax.sharding import PartitionSpec as P

CAP = 48
TOP = 8
TOK = 128
D = 2048
HID = 192
DS = 512
EPS = 1e-06
CA = 3
CR = 3
MESH = pl.DeviceIdType.MESH
BF = jnp.bfloat16
F32 = jnp.float32


def dot_tt(a, b):
    return lax.dot_general(a, b, (((0,), (0,)), ((), ())), preferred_element_type=F32)


def dot_nt(a, b):
    return lax.dot_general(a, b, (((1,), (1,)), ((), ())), preferred_element_type=F32)


def dot_nn(a, b):
    return jnp.dot(a, b, preferred_element_type=F32)


def tables(chosen, weights):
    chosen, weights = chosen.T, weights.T
    picked = chosen == 0
    routed = jnp.max(picked.astype(F32), axis=1, keepdims=True)
    scale = jnp.sum(jnp.where(picked, weights, 0.0), axis=1, keepdims=True)
    row = lax.broadcasted_iota(jnp.int32, (TOK, TOK), 0)
    col = lax.broadcasted_iota(jnp.int32, (TOK, TOK), 1)
    lower = (col <= row).astype(BF)
    count = dot_nn(lower, jnp.broadcast_to(routed, (TOK, TOK)).astype(BF))[:, :1]
    slot = jnp.where(routed > 0.5, count - 1.0, -1.0)
    place = lax.broadcasted_iota(jnp.int32, (TOK, 4 * CAP), 1)
    place = (
        place
        - CAP * (place >= CAP).astype(jnp.int32)
        - CAP * (place >= 2 * CAP).astype(jnp.int32)
        - CAP * (place >= 3 * CAP).astype(jnp.int32)
    )
    table = jnp.where(slot == place.astype(F32), 1.0, 0.0).astype(BF)
    return table, scale


def slots(chosen, weights):
    picked = chosen == 0
    routed = jnp.max(picked.astype(F32), axis=0, keepdims=True)
    scale = jnp.sum(jnp.where(picked, weights, 0.0), axis=0, keepdims=True)
    row = lax.broadcasted_iota(jnp.int32, (TOK, TOK), 0)
    col = lax.broadcasted_iota(jnp.int32, (TOK, TOK), 1)
    upper = (row <= col).astype(BF)
    count = dot_nn(jnp.broadcast_to(routed, (TOP, TOK)).astype(BF), upper)[:1]
    slot = jnp.where(routed > 0.5, count - 1.0, -1.0)
    hit = slot == lax.broadcasted_iota(jnp.int32, (CAP, TOK), 0).astype(F32)
    return jnp.where(hit, 1.0, 0.0).astype(BF), jnp.sum(jnp.where(hit, scale, 0.0), axis=1, keepdims=True)


def inverse_rms(x):
    return lax.rsqrt(jnp.mean(x * x, axis=1, keepdims=True) + EPS)


def sigmoid(v):
    return 1.0 / (1.0 + jnp.exp(-v))


def kernel(
    so_ref, ft_ref, kept_ref, sc_ref, lc_ref, gain_in, gw_ref, uw_ref, dw_ref, fe_in, fs_in, be_in, bs_in,
    lo_ref, ig_ref, gg_ref, ug_ref, dg_ref, gt_ref,
    fe_ref, fs_ref, be_ref, bs_ref, gain_ref, kept, cot, inc, w, rows, part, got, mid, relay, acts, dwst, dwmid, dwgot, dwout, lo, ig, gst, gout,
    lsem, osem, ssem, srsem, wsend, wrecv, zsend, zrecv, psend, precv, csend, crecv, rsem, ready, dsend, drecv, gsend, grecv,
):
    s, e, r = lax.axis_index("section"), lax.axis_index("expert"), lax.axis_index("dp")
    last = lax.axis_size("section") - 1
    inner = (e == 1) | (e == 2)
    outer = jnp.logical_not(inner)
    end = jnp.where(e == 1, 0, 3)
    other = 3 - e
    far = 3 - end
    near = jnp.where(e == 0, 1, 2)

    def remote(src, dst, ss, rs, dev):
        return pltpu.make_async_remote_copy(
            src_ref=src, dst_ref=dst, send_sem=ss, recv_sem=rs, device_id=dev, device_id_type=MESH
        )

    xs = [lax.rem(r + d, 4) for d in range(4)]
    zs = [lax.rem(e + d, 4) for d in range(4)]

    own_w = [pltpu.make_async_copy(ref, w.at[a, r], lsem.at[1 + a]) for a, ref in enumerate((gw_ref, uw_ref, dw_ref))]
    load_kept = pltpu.make_async_copy(kept_ref, kept, lsem.at[0])
    smalls = [
        pltpu.make_async_copy(src, dst, lsem.at[6 + i])
        for i, (src, dst) in enumerate(
            ((be_in, be_ref), (bs_in, bs_ref), (gain_in, gain_ref), (fe_in, fe_ref), (fs_in, fs_ref))
        )
    ]
    smalls[0].start()
    smalls[1].start()
    load_kept.start()
    for c in smalls[2:]:
        c.start()
    barrier = pltpu.get_barrier_semaphore()
    for d in (1, 3):
        pl.semaphore_signal(barrier, inc=1, device_id=(s, e, xs[d]), device_id_type=MESH)

    @pl.when(outer)
    def _():
        pl.semaphore_signal(barrier, inc=1, device_id=(s, near, r), device_id_type=MESH)

    @pl.when(inner)
    def _():
        pl.semaphore_signal(barrier, inc=1, device_id=(s, other, r), device_id_type=MESH)
        pl.semaphore_signal(barrier, inc=1, device_id=(s, end, r), device_id_type=MESH)

    from_next = (s < last) & (s != last // 2)
    from_before = (s > 0) & (s != last // 2 + 1)

    @pl.when(from_next)
    def _():
        pl.semaphore_signal(barrier, inc=1, device_id=(s + 1, e, r), device_id_type=MESH)

    @pl.when(from_before)
    def _():
        pl.semaphore_signal(barrier, inc=1, device_id=(s - 1, e, r), device_id_type=MESH)

    half = (last + 1) // 2
    relays = half // 2
    up_relay = (s > half) & (lax.rem(s, 2) == 1)
    down_relay = (s < half) & (lax.rem(s, 2) == 0)
    relay_at = jnp.where(s > half, s - half, s) // 2

    @pl.when(down_relay)
    def _():
        pl.semaphore_signal(barrier, inc=1, device_id=(half, e, r), device_id_type=MESH)

    @pl.when(s == half)
    def _():
        for k in range(relays):
            pl.semaphore_signal(barrier, inc=1, device_id=(half + 1 + 2 * k, e, r), device_id_type=MESH)

    @pl.when(s == half - 1)
    def _():
        for k in range(relays):
            pl.semaphore_signal(barrier, inc=1, device_id=(2 * k, e, r), device_id_type=MESH)
            pl.semaphore_signal(barrier, inc=1, device_id=(half + 1 + 2 * k, e, r), device_id_type=MESH)

    for c in own_w:
        c.start()
    first_in = pltpu.make_async_copy(ft_ref, inc, lsem.at[4])
    loss_in = pltpu.make_async_copy(lc_ref, cot, lsem.at[5])

    @pl.when(s == 0)
    def _():
        first_in.start()

    @pl.when(s == last)
    def _():
        loss_in.start()

    one, none = jnp.int32(1), jnp.int32(0)
    pl.semaphore_wait(
        barrier,
        3
        + jnp.where(inner, one, none)
        + jnp.where(from_next, one, none)
        + jnp.where(from_before, one, none)
        + jnp.where(up_relay, 2, 0)
        + jnp.where(down_relay, one, none)
        + jnp.where(s == half, relays, 0),
    )

    @pl.when(up_relay)
    def _():
        pl.semaphore_signal(ready, inc=1, device_id=(half - 1, e, r), device_id_type=MESH)

    hop_cot = remote(sc_ref, cot, ssem.at[0], srsem.at[0], (jnp.maximum(s - 1, 0), e, r))
    hop_inc = remote(so_ref, inc, ssem.at[1], srsem.at[1], (jnp.minimum(s + 1, last), e, r))

    @pl.when(from_before)
    def _():
        hop_cot.start()

    @pl.when(from_next)
    def _():
        hop_inc.start()

    step = TOK // relays

    def out_by(ref, k, section):
        return remote(ref.at[pl.ds(k * step, step)], relay, csend.at[k], rsem.at[0], (section, e, r))

    @pl.when(s == half)
    def _():
        for k in range(relays):
            out_by(sc_ref, k, 2 * k).start()

    def out_up():
        pl.semaphore_wait(ready, relays)
        for k in range(relays):
            out_by(so_ref, k, half + 1 + 2 * k).start()

    def in_by(dst, k, section):
        first = k * step if isinstance(k, int) else pl.multiple_of(k * step, step)
        return remote(relay, dst.at[pl.ds(first, step)], rsem.at[1], crecv.at[k], (section, e, r))

    def pass_relay():
        @pl.when(up_relay)
        def _():
            c = in_by(inc, relay_at, half)
            out_by(so_ref, 0, half).wait_recv()
            c.start()

        @pl.when(down_relay)
        def _():
            c = in_by(cot, relay_at, half - 1)
            out_by(sc_ref, 0, half).wait_recv()
            c.start()

    right, left = (s, e, xs[1]), (s, e, xs[3])
    up_half, low_half = pl.ds(0, HID // 2), pl.ds(HID // 2, HID // 2)
    w_refs = (gw_ref, uw_ref, dw_ref)

    def w_right(a, slot):
        return remote(w_refs[a], w.at[a, slot], wsend.at[a, 0], wrecv.at[a, 0], right)

    def w_left(a, slot):
        return remote(w_refs[a], w.at[a, slot], wsend.at[a, 1], wrecv.at[a, 1], left)

    def w_right_on(a, slot):
        ref = w.at[a, slot, up_half]
        return remote(ref, ref, wsend.at[a, 2], wrecv.at[a, 2], right)

    def w_left_on(a, slot):
        ref = w.at[a, slot, low_half]
        return remote(ref, ref, wsend.at[a, 3], wrecv.at[a, 3], left)

    for a in range(3):
        w_right(a, r).start()
        w_left(a, r).start()

    def w_pass(a):
        w_right(a, xs[3]).wait_recv()
        w_right_on(a, xs[3]).start()
        w_left(a, xs[1]).wait_recv()
        w_left_on(a, xs[1]).start()

    def w_arrived(a):
        own_w[a].wait()
        w_right_on(a, xs[2]).wait_recv()
        w_left_on(a, xs[2]).wait_recv()

    def w_sent(a):
        for make in (w_right, w_left, w_right_on, w_left_on):
            make(a, r).wait_send()

    ca = CAP // CA

    def z_copy(a, block, k, dev, c):
        ref = rows.at[a, block, pl.ds(c * ca, ca)]
        return remote(ref, ref, zsend.at[a, k, c], zrecv.at[a, block, c], (s, dev, r))

    def z_send(a, k, dev):
        for c in range(CA):
            z_copy(a, e, k, dev, c).start()

    def z_own(a):
        @pl.when(inner)
        def _():
            for c in range(CA):
                z_copy(a, e, 0, other, c).start()
                z_copy(a, e, 1, end, c).start()

        @pl.when(outer)
        def _():
            z_send(a, 0, near)

    def z_pass(a, *moves):
        @pl.when(inner)
        def _():
            for c in range(CA):
                for block, k, dev in moves:
                    copy = z_copy(a, block, k, dev, c)
                    copy.wait_recv()
                    copy.start()

    def normed_rows(pick, tokens):
        x = dot_nn(pick, tokens)
        return (x * inverse_rms(x) * gain_ref[...]).astype(BF)

    smalls[0].wait()
    smalls[1].wait()
    pick_b, pick_scale = slots(be_ref[...], bs_ref[...])
    load_kept.wait()
    smalls[2].wait()
    rows[0, e] = normed_rows(pick_b, kept[...])
    z_own(0)
    smalls[3].wait()
    smalls[4].wait()
    pick_f, _ = slots(fe_ref[...], fs_ref[...])
    z_pass(0, (end, 2, other), (other, 3, end))
    w_pass(0)

    late = s == half - 1
    punctual = jnp.logical_not(late)

    @pl.when(late)
    def _():
        w_pass(1)
        z_pass(0, (far, 4, end))
        hop_inc.wait_recv()
        rows[2, e] = normed_rows(pick_f, inc[...])
        z_own(2)
        out_up()

    @pl.when(s == last)
    def _():
        loss_in.wait()

    @pl.when(s == half - 1)
    def _():
        for k in range(relays):
            in_by(cot, k, half - 1).wait_recv()

    @pl.when(from_next)
    def _():
        hop_cot.wait_recv()

    rows[1, e] = (pick_scale * dot_nn(pick_b, cot[...])).astype(BF)
    z_own(1)

    @pl.when(punctual)
    def _():
        w_pass(1)
        z_pass(0, (far, 4, end))

    pass_relay()

    @pl.when(s == 0)
    def _():
        first_in.wait()

    @pl.when(from_before & punctual)
    def _():
        hop_inc.wait_recv()

    @pl.when(punctual & (s != half))
    def _():
        rows[2, e] = normed_rows(pick_f, inc[...])

    @pl.when(outer & punctual & (s != half))
    def _():
        z_send(2, 0, near)

    z_pass(1, (end, 2, other), (other, 3, end))
    w_pass(2)

    @pl.when(s != half)
    def _():
        z_pass(2, (end, 2, other))

    @pl.when(inner & punctual & (s != half))
    def _():
        z_send(2, 0, other)

    z_pass(1, (far, 4, end))

    @pl.when(s == half)
    def _():
        for k in range(relays):
            in_by(inc, k, half).wait_recv()
        rows[2, e] = normed_rows(pick_f, inc[...])

        @pl.when(outer)
        def _():
            z_send(2, 0, near)

        z_pass(2, (end, 2, other))

        @pl.when(inner)
        def _():
            z_send(2, 0, other)

    def z_arrived(a, block):
        for c in range(CA):
            z_copy(a, block, 0, near, c).wait_recv()

    def project(a, group):
        total = None
        for k in range(4):
            prod = dot_nt(group[:, k * DS : (k + 1) * DS], w[a, k])
            total = prod if total is None else total + prod
        return total

    def backward_acts(group_in, group_grad):
        gate_act = project(0, group_in)
        up_act = project(1, group_in)
        squash = sigmoid(gate_act)
        act = gate_act * squash
        grad_hidden = project(2, group_grad)
        return (
            (grad_hidden * up_act * squash * (1.0 + gate_act * (1.0 - squash))).astype(BF),
            (grad_hidden * act).astype(BF),
            (act * up_act).astype(BF),
        )

    def forward_acts(group):
        g = project(0, group)
        return (g * sigmoid(g) * project(1, group)).astype(BF)

    def backward_part(grad_gate, grad_up, k):
        return (dot_nn(grad_gate, w[0, k]) + dot_nn(grad_up, w[1, k])).astype(BF)

    def forward_part(hidden, k):
        return dot_nn(hidden, w[2, k]).astype(BF)

    def backward_block(block):
        made = backward_acts(rows[0, block], rows[1, block])
        for a in range(3):
            acts[a, block] = made[a]
        for k in range(4):
            part[0, block, :, k * DS : (k + 1) * DS] = backward_part(made[0], made[1], k)

    def forward_block(block):
        hidden = forward_acts(rows[2, block])
        for k in range(4):
            part[1, block, :, k * DS : (k + 1) * DS] = forward_part(hidden, k)

    cr = CAP // CR

    def leg(j, src, dst, k, m, dev, c):
        return remote(src, dst.at[pl.ds(c * cr, cr)], psend.at[j, k, c], precv.at[j, m, c], (s, dev, r))

    def for_far(j, c):
        return leg(j, part.at[j, 3 - e, pl.ds(c * cr, cr)], mid.at[j, 0], 0, 0, near, c)

    def for_across(j, c):
        return leg(j, part.at[j, 3 - near, pl.ds(c * cr, cr)], mid.at[j, 1], 1, 1, near, c)

    def for_near(j, c):
        return leg(j, part.at[j, near, pl.ds(c * cr, cr)], got.at[j, 1], 2, 2, near, c)

    def on_far(j, c):
        return leg(j, part.at[j, far, pl.ds(c * cr, cr)], mid.at[j, 2], 0, 3, other, c)

    def on_other(j, c):
        return leg(j, part.at[j, other, pl.ds(c * cr, cr)], got.at[j, 2], 1, 4, other, c)

    def on_end(j, c):
        return leg(j, part.at[j, end, pl.ds(c * cr, cr)], got.at[j, 1], 2, 2, end, c)

    def add_mid(j, dest, m, c):
        here = pl.ds(c * cr, cr)
        part[j, dest, here, :] = (part[j, dest, here, :].astype(F32) + mid[j, m, here, :].astype(F32)).astype(BF)

    def pass_term(j, dest, m, arriving, leaving):
        for c in range(CR):
            arriving(j, c).wait_recv()
            add_mid(j, dest, m, c)
            leaving(j, c).start()

    def send_term(j, make):
        for c in range(CR):
            make(j, c).start()

    def parts_arrived(j):
        for c in range(CR):
            for_near(j, c).wait_recv()

        @pl.when(inner)
        def _():
            for c in range(CR):
                on_other(j, c).wait_recv()

    def parts_sent(j):
        for k in range(3):
            for c in range(CR):
                leg(j, part.at[j, 0, pl.ds(c * cr, cr)], mid.at[j, 0], k, 0, near, c).wait_send()

    def d_far(a, h):
        half_rows = (up_half, low_half)[h]
        return remote(
            dwst.at[a, xs[2], half_rows], dwmid.at[a, h], dsend.at[a, h], drecv.at[a, h], (right, left)[h]
        )

    def d_near(a, h, joined):
        half_rows = (up_half, low_half)[h if joined else 1 - h]
        n = 2 + 2 * h + (1 if joined else 0)
        return remote(
            dwst.at[a, (xs[1], xs[3])[h], half_rows],
            dwgot.at[a, h, half_rows],
            dsend.at[a, n],
            drecv.at[a, n],
            (right, left)[h],
        )

    def send_weight_grads():
        group_in, group_grad = rows[0].reshape(4 * CAP, D), rows[1].reshape(4 * CAP, D)
        for a, group in enumerate((group_in, group_in, group_grad)):
            act = acts[a].reshape(4 * CAP, HID)
            for k in range(4):
                dwst[a, k] = dot_tt(act, group[:, k * DS : (k + 1) * DS]).astype(BF)
            for h in range(2):
                d_far(a, h).start()

    def send_weight_grads_near():
        for a in range(3):
            for h in range(2):
                d_near(a, h, False).start()

    def join_weight_grads():
        for a in range(3):
            for h in range(2):
                d_far(a, h).wait_recv()
                half_rows, to = (up_half, low_half)[h], (xs[1], xs[3])[h]
                joined = dwst[a, to, half_rows, :].astype(F32) + dwmid[a, h].astype(F32)
                dwst[a, to, half_rows, :] = joined.astype(BF)
                d_near(a, h, True).start()

    gain = gain_ref[...]
    table_b, scale_b = tables(be_ref[...], bs_ref[...])
    table_f, scale_f = tables(fe_ref[...], fs_ref[...])
    rscale_b = inverse_rms(kept[...].astype(F32))

    for a in range(3):
        w_arrived(a)

    gain_z = [remote(gst.at[0, 0], gst.at[0, d], gsend.at[0, d], grecv.at[0, d], (s, zs[d], r)) for d in (1, 2, 3)]
    gain_x = [remote(gst.at[1, 0], gst.at[1, d], gsend.at[1, d], grecv.at[1, d], (s, e, xs[d])) for d in (1, 2, 3)]

    def send_gain():
        terms = part[0].reshape(4 * CAP, D).astype(F32) * rows[0].reshape(4 * CAP, D).astype(F32)
        gst[0, 0] = jnp.sum(terms, axis=0, keepdims=True) / gain
        for c in gain_z:
            c.start()

    def pass_gain():
        for c in gain_z:
            c.wait_recv()
        gst[1, 0] = (gst[0, 0] + gst[0, 1]) + (gst[0, 2] + gst[0, 3])
        for c in gain_x:
            c.start()

    @pl.when(outer)
    def _():
        got[0, 2] = jnp.zeros((CAP, D), BF)
        got[1, 2] = jnp.zeros((CAP, D), BF)
        for block, make in ((near, for_near), (3 - near, for_across), (3 - e, for_far)):
            z_arrived(0, block)
            z_arrived(1, block)
            backward_block(block)
            send_term(0, make)
            if make is for_near:
                backward_block(e)
        send_weight_grads()
        send_gain()
        for block, make in ((3 - e, for_far), (3 - near, for_across), (near, for_near)):
            z_arrived(2, block)
            forward_block(block)
            send_term(1, make)
            if make is for_far:
                send_weight_grads_near()
                forward_block(e)
            if make is for_across:
                join_weight_grads()
                pass_gain()

    @pl.when(inner)
    def _():
        made = backward_acts(rows[0].reshape(4 * CAP, D), rows[1].reshape(4 * CAP, D))
        for a in range(3):
            acts[a] = made[a].reshape(4, CAP, HID)
        for k in range(4):
            part[0, :, :, k * DS : (k + 1) * DS] = backward_part(made[0], made[1], k).reshape(4, CAP, DS)
        send_weight_grads()
        send_gain()

    z_pass(2, (far, 4, end))
    z_pass(2, (other, 3, end))

    @pl.when(inner & punctual)
    def _():
        z_send(2, 1, end)

    @pl.when(inner)
    def _():
        hidden = forward_acts(rows[2].reshape(4 * CAP, D))
        for k in range(4):
            part[1, :, :, k * DS : (k + 1) * DS] = forward_part(hidden, k).reshape(4, CAP, DS)
        send_weight_grads_near()
        pass_term(0, other, 1, for_across, on_other)
        join_weight_grads()
        pass_term(0, far, 0, for_far, on_far)
        pass_gain()
        pass_term(0, end, 2, on_far, on_end)
        pass_term(1, far, 0, for_far, on_far)

    got[0, 0] = part[0, e]
    got[1, 0] = part[1, e]

    parts_arrived(0)
    grad_normed = dot_nn(table_b[:, : 3 * CAP], got[0].reshape(3 * CAP, D))
    xhat = kept[...].astype(F32) * rscale_b
    gx = grad_normed * gain
    mean = jnp.mean(gx * xhat, axis=1, keepdims=True)
    ig[...] = (cot[...].astype(F32) + rscale_b * (gx - xhat * mean)).astype(BF)
    out_ig = pltpu.make_async_copy(ig, ig_ref, osem.at[0])
    out_ig.start()

    @pl.when(inner)
    def _():
        pass_term(1, other, 1, for_across, on_other)
        pass_term(1, end, 2, on_far, on_end)

    outs = [out_ig]
    for a, ref in enumerate((gg_ref, ug_ref, dg_ref)):
        for h in range(2):
            d_near(a, h, False).wait_recv()
            d_near(a, h, True).wait_recv()
        total = dwst[a, r].astype(F32) + (dwgot[a, 0].astype(F32) + dwgot[a, 1].astype(F32))
        dwout[a] = total.astype(BF)
        c = pltpu.make_async_copy(dwout.at[a], ref, osem.at[2 + a])
        c.start()
        outs.append(c)
    parts_arrived(1)
    tokens = dot_nn(table_f[:, : 3 * CAP], got[1].reshape(3 * CAP, D))
    lo[...] = (inc[...].astype(F32) + scale_f * tokens).astype(BF)
    out_lo = pltpu.make_async_copy(lo, lo_ref, osem.at[1])
    out_lo.start()
    outs.append(out_lo)

    for c in gain_x:
        c.wait_recv()
    gout[...] = (gst[1, 0] + gst[1, 1]) + (gst[1, 2] + gst[1, 3])
    c = pltpu.make_async_copy(gout, gt_ref, osem.at[5])
    c.start()
    outs.append(c)

    @pl.when(from_before)
    def _():
        hop_cot.wait_send()

    @pl.when(from_next)
    def _():
        hop_inc.wait_send()

    @pl.when((s == half) | (s == half - 1))
    def _():
        for k in range(relays):
            out_by(so_ref, k, half).wait_send()

    @pl.when(up_relay | down_relay)
    def _():
        in_by(inc, 0, half).wait_send()

    parts_sent(0)
    parts_sent(1)

    for a in range(3):
        w_sent(a)
        for h in range(2):
            d_far(a, h).wait_send()
            d_near(a, h, False).wait_send()
            d_near(a, h, True).wait_send()
    for c in gain_z + gain_x:
        c.wait_send()
    for a in range(3):
        for c in range(CA):
            z_copy(a, e, 0, near, c).wait_send()

        @pl.when(inner)
        def _():
            for k in range(1, 5):
                for c in range(CA):
                    z_copy(a, e, k, end, c).wait_send()

    for c in outs:
        c.wait()


def finish(*refs):
    copies = [pltpu.make_async_copy(refs[i], refs[6 + i], refs[12].at[i]) for i in range(6)]
    for c in copies:
        c.start()
    for c in copies:
        c.wait()


def local(so, ft, kept, sc, lc, gain, gw, uw, dw, fe, fs, be, bs):
    any_spec = pl.BlockSpec(memory_space=pl.ANY)
    dma = pltpu.SemaphoreType.DMA
    hbm = lambda x: pltpu.with_memory_space_constraint(x, pltpu.HBM)
    outs = pl.pallas_call(
        kernel,
        out_shape=(
            jax.ShapeDtypeStruct((TOK, D), BF),
            jax.ShapeDtypeStruct((TOK, D), BF),
            jax.ShapeDtypeStruct((HID, DS), BF),
            jax.ShapeDtypeStruct((HID, DS), BF),
            jax.ShapeDtypeStruct((HID, DS), BF),
            jax.ShapeDtypeStruct((1, D), F32),
        ),
        in_specs=[any_spec] * 13,
        out_specs=[any_spec] * 6,
        scratch_shapes=[
            pltpu.VMEM((TOP, TOK), jnp.int32),
            pltpu.VMEM((TOP, TOK), F32),
            pltpu.VMEM((TOP, TOK), jnp.int32),
            pltpu.VMEM((TOP, TOK), F32),
            pltpu.VMEM((1, D), F32),
            pltpu.VMEM((TOK, D), BF),
            pltpu.VMEM((TOK, D), BF),
            pltpu.VMEM((TOK, D), BF),
            pltpu.VMEM((3, 4, HID, DS), BF),
            pltpu.VMEM((3, 4, CAP, D), BF),
            pltpu.VMEM((2, 4, CAP, D), BF),
            pltpu.VMEM((2, 3, CAP, D), BF),
            pltpu.VMEM((2, 3, CAP, D), BF),
            pltpu.VMEM((16, D), BF),
            pltpu.VMEM((3, 4, CAP, HID), BF),
            pltpu.VMEM((3, 4, HID, DS), BF),
            pltpu.VMEM((3, 2, HID // 2, DS), BF),
            pltpu.VMEM((3, 2, HID, DS), BF),
            pltpu.VMEM((3, HID, DS), BF),
            pltpu.VMEM((TOK, D), BF),
            pltpu.VMEM((TOK, D), BF),
            pltpu.VMEM((2, 4, 1, D), F32),
            pltpu.VMEM((1, D), F32),
            dma((11,)),
            dma((6,)),
            dma((2,)),
            dma((2,)),
            dma((3, 4)),
            dma((3, 4)),
            dma((3, 5, CA)),
            dma((3, 4, CA)),
            dma((2, 3, CR)),
            dma((2, 5, CR)),
            dma((8,)),
            dma((8,)),
            dma((2,)),
            pltpu.SemaphoreType.REGULAR,
            dma((3, 6)),
            dma((3, 6)),
            dma((2, 4)),
            dma((2, 4)),
        ],
        compiler_params=pltpu.CompilerParams(
            collective_id=0, has_side_effects=True, vmem_limit_bytes=40 << 20
        ),
        name="relay",
    )(
        hbm(so.reshape(TOK, D)), hbm(ft.reshape(TOK, D)), hbm(kept.reshape(TOK, D)), hbm(sc.reshape(TOK, D)),
        hbm(lc.reshape(TOK, D)), hbm(gain.reshape(1, D)), hbm(gw[0]), hbm(uw[0]), hbm(dw[0]),
        hbm(fe[0, 0].T), hbm(fs[0, 0].T), hbm(be[0, 0].T), hbm(bs[0, 0].T),
    )
    outs = pl.pallas_call(
        finish,
        out_shape=tuple(jax.ShapeDtypeStruct(o.shape, o.dtype) for o in outs),
        in_specs=[any_spec] * 6,
        out_specs=[any_spec] * 6,
        scratch_shapes=[dma((6,))],
        compiler_params=pltpu.CompilerParams(vmem_limit_bytes=16 << 20),
        name="finish",
    )(*[pltpu.with_memory_space_constraint(o, pltpu.VMEM) for o in outs])
    return (
        outs[0][None, None], outs[1][None, None], outs[2][None], outs[3][None], outs[4][None], outs[5],
    )


def solution(mesh):
    tokens = P("section", "dp", "expert", None)
    stored = P("section", "expert", "dp")
    first = P("dp", "expert", None)
    return jax.shard_map(
        local,
        mesh=mesh,
        in_specs=(tokens, first, tokens, tokens, first, P("section", None)) + (stored,) * 3 + (tokens,) * 4,
        out_specs=(tokens, tokens, stored, stored, stored, P("section", None)),
        check_vma=False,
    )
```

```python
import jax
import jax.numpy as jnp
from jax import lax
from jax.experimental import pallas as pl
from jax.experimental.pallas import tpu as pltpu
from jax.sharding import PartitionSpec as P

CAP = 48
TOP = 8
TOK = 128
D = 2048
HID = 192
DS = 512
EPS = 1e-06
CA = 3
CR = 3
MESH = pl.DeviceIdType.MESH
BF = jnp.bfloat16
F32 = jnp.float32


def dot_tt(a, b):
    return lax.dot_general(a, b, (((0,), (0,)), ((), ())), preferred_element_type=F32)


def dot_nt(a, b):
    return lax.dot_general(a, b, (((1,), (1,)), ((), ())), preferred_element_type=F32)


def dot_nn(a, b):
    return jnp.dot(a, b, preferred_element_type=F32)


def tables(chosen, weights):
    chosen, weights = chosen.T, weights.T
    picked = chosen == 0
    routed = jnp.max(picked.astype(F32), axis=1, keepdims=True)
    scale = jnp.sum(jnp.where(picked, weights, 0.0), axis=1, keepdims=True)
    row = lax.broadcasted_iota(jnp.int32, (TOK, TOK), 0)
    col = lax.broadcasted_iota(jnp.int32, (TOK, TOK), 1)
    lower = (col <= row).astype(BF)
    count = dot_nn(lower, jnp.broadcast_to(routed, (TOK, TOK)).astype(BF))[:, :1]
    slot = jnp.where(routed > 0.5, count - 1.0, -1.0)
    place = lax.broadcasted_iota(jnp.int32, (TOK, 4 * CAP), 1)
    place = (
        place
        - CAP * (place >= CAP).astype(jnp.int32)
        - CAP * (place >= 2 * CAP).astype(jnp.int32)
        - CAP * (place >= 3 * CAP).astype(jnp.int32)
    )
    table = jnp.where(slot == place.astype(F32), 1.0, 0.0).astype(BF)
    return table, scale


def slots(chosen, weights):
    picked = chosen == 0
    routed = jnp.max(picked.astype(F32), axis=0, keepdims=True)
    scale = jnp.sum(jnp.where(picked, weights, 0.0), axis=0, keepdims=True)
    row = lax.broadcasted_iota(jnp.int32, (TOK, TOK), 0)
    col = lax.broadcasted_iota(jnp.int32, (TOK, TOK), 1)
    upper = (row <= col).astype(BF)
    count = dot_nn(jnp.broadcast_to(routed, (TOP, TOK)).astype(BF), upper)[:1]
    slot = jnp.where(routed > 0.5, count - 1.0, -1.0)
    hit = slot == lax.broadcasted_iota(jnp.int32, (CAP, TOK), 0).astype(F32)
    return jnp.where(hit, 1.0, 0.0).astype(BF), jnp.sum(jnp.where(hit, scale, 0.0), axis=1, keepdims=True)


def inverse_rms(x):
    return lax.rsqrt(jnp.mean(x * x, axis=1, keepdims=True) + EPS)


def sigmoid(v):
    return 1.0 / (1.0 + jnp.exp(-v))


def kernel(
    so_ref, ft_ref, kept_ref, sc_ref, lc_ref, gain_in, gw_ref, uw_ref, dw_ref, fe_in, fs_in, be_in, bs_in,
    lo_ref, ig_ref, gg_ref, ug_ref, dg_ref, gt_ref,
    fe_ref, fs_ref, be_ref, bs_ref, gain_ref, kept, cot, inc, w, rows, part, got, mid, relay, acts, dwst, dwmid, dwgot, dwout, lo, ig, gst, gout,
    lsem, osem, ssem, srsem, wsend, wrecv, zsend, zrecv, psend, precv, csend, crecv, rsem, ready, dsend, drecv, gsend, grecv,
):
    s, e, r = lax.axis_index("section"), lax.axis_index("expert"), lax.axis_index("dp")
    last = lax.axis_size("section") - 1
    inner = (e == 1) | (e == 2)
    outer = jnp.logical_not(inner)
    end = jnp.where(e == 1, 0, 3)
    other = 3 - e
    far = 3 - end
    near = jnp.where(e == 0, 1, 2)

    def remote(src, dst, ss, rs, dev):
        return pltpu.make_async_remote_copy(
            src_ref=src, dst_ref=dst, send_sem=ss, recv_sem=rs, device_id=dev, device_id_type=MESH
        )

    xs = [lax.rem(r + d, 4) for d in range(4)]
    zs = [lax.rem(e + d, 4) for d in range(4)]

    own_w = [pltpu.make_async_copy(ref, w.at[a, r], lsem.at[1 + a]) for a, ref in enumerate((gw_ref, uw_ref, dw_ref))]
    load_kept = pltpu.make_async_copy(kept_ref, kept, lsem.at[0])
    smalls = [
        pltpu.make_async_copy(src, dst, lsem.at[6 + i])
        for i, (src, dst) in enumerate(
            ((be_in, be_ref), (bs_in, bs_ref), (gain_in, gain_ref), (fe_in, fe_ref), (fs_in, fs_ref))
        )
    ]
    smalls[0].start()
    smalls[1].start()
    load_kept.start()
    for c in smalls[2:]:
        c.start()
    barrier = pltpu.get_barrier_semaphore()
    for d in (1, 3):
        pl.semaphore_signal(barrier, inc=1, device_id=(s, e, xs[d]), device_id_type=MESH)

    @pl.when(outer)
    def _():
        pl.semaphore_signal(barrier, inc=1, device_id=(s, near, r), device_id_type=MESH)

    @pl.when(inner)
    def _():
        pl.semaphore_signal(barrier, inc=1, device_id=(s, other, r), device_id_type=MESH)
        pl.semaphore_signal(barrier, inc=1, device_id=(s, end, r), device_id_type=MESH)

    from_next = (s < last) & (s != last // 2)
    from_before = (s > 0) & (s != last // 2 + 1)

    @pl.when(from_next)
    def _():
        pl.semaphore_signal(barrier, inc=1, device_id=(s + 1, e, r), device_id_type=MESH)

    @pl.when(from_before)
    def _():
        pl.semaphore_signal(barrier, inc=1, device_id=(s - 1, e, r), device_id_type=MESH)

    half = (last + 1) // 2
    relays = half // 2
    up_relay = (s > half) & (lax.rem(s, 2) == 1)
    down_relay = (s < half) & (lax.rem(s, 2) == 0)
    relay_at = jnp.where(s > half, s - half, s) // 2

    @pl.when(down_relay)
    def _():
        pl.semaphore_signal(barrier, inc=1, device_id=(half, e, r), device_id_type=MESH)

    @pl.when(s == half)
    def _():
        for k in range(relays):
            pl.semaphore_signal(barrier, inc=1, device_id=(half + 1 + 2 * k, e, r), device_id_type=MESH)

    @pl.when(s == half - 1)
    def _():
        for k in range(relays):
            pl.semaphore_signal(barrier, inc=1, device_id=(2 * k, e, r), device_id_type=MESH)
            pl.semaphore_signal(barrier, inc=1, device_id=(half + 1 + 2 * k, e, r), device_id_type=MESH)

    for c in own_w:
        c.start()
    first_in = pltpu.make_async_copy(ft_ref, inc, lsem.at[4])
    loss_in = pltpu.make_async_copy(lc_ref, cot, lsem.at[5])

    @pl.when(s == 0)
    def _():
        first_in.start()

    @pl.when(s == last)
    def _():
        loss_in.start()

    one, none = jnp.int32(1), jnp.int32(0)
    pl.semaphore_wait(
        barrier,
        3
        + jnp.where(inner, one, none)
        + jnp.where(from_next, one, none)
        + jnp.where(from_before, one, none)
        + jnp.where(up_relay, 2, 0)
        + jnp.where(down_relay, one, none)
        + jnp.where(s == half, relays, 0),
    )

    @pl.when(up_relay)
    def _():
        pl.semaphore_signal(ready, inc=1, device_id=(half - 1, e, r), device_id_type=MESH)

    hop_cot = remote(sc_ref, cot, ssem.at[0], srsem.at[0], (jnp.maximum(s - 1, 0), e, r))
    hop_inc = remote(so_ref, inc, ssem.at[1], srsem.at[1], (jnp.minimum(s + 1, last), e, r))

    @pl.when(from_before)
    def _():
        hop_cot.start()

    @pl.when(from_next)
    def _():
        hop_inc.start()

    step = TOK // relays

    def out_by(ref, k, section):
        return remote(ref.at[pl.ds(k * step, step)], relay, csend.at[k], rsem.at[0], (section, e, r))

    @pl.when(s == half)
    def _():
        for k in range(relays):
            out_by(sc_ref, k, 2 * k).start()

    def out_up():
        pl.semaphore_wait(ready, relays)
        for k in range(relays):
            out_by(so_ref, k, half + 1 + 2 * k).start()

    def in_by(dst, k, section):
        first = k * step if isinstance(k, int) else pl.multiple_of(k * step, step)
        return remote(relay, dst.at[pl.ds(first, step)], rsem.at[1], crecv.at[k], (section, e, r))

    def pass_relay():
        @pl.when(up_relay)
        def _():
            c = in_by(inc, relay_at, half)
            out_by(so_ref, 0, half).wait_recv()
            c.start()

        @pl.when(down_relay)
        def _():
            c = in_by(cot, relay_at, half - 1)
            out_by(sc_ref, 0, half).wait_recv()
            c.start()

    right, left = (s, e, xs[1]), (s, e, xs[3])
    up_half, low_half = pl.ds(0, HID // 2), pl.ds(HID // 2, HID // 2)
    w_refs = (gw_ref, uw_ref, dw_ref)

    def w_right(a, slot):
        return remote(w_refs[a], w.at[a, slot], wsend.at[a, 0], wrecv.at[a, 0], right)

    def w_left(a, slot):
        return remote(w_refs[a], w.at[a, slot], wsend.at[a, 1], wrecv.at[a, 1], left)

    def w_right_on(a, slot):
        ref = w.at[a, slot, up_half]
        return remote(ref, ref, wsend.at[a, 2], wrecv.at[a, 2], right)

    def w_left_on(a, slot):
        ref = w.at[a, slot, low_half]
        return remote(ref, ref, wsend.at[a, 3], wrecv.at[a, 3], left)

    for a in range(3):
        w_right(a, r).start()
        w_left(a, r).start()

    def w_pass(a):
        w_right(a, xs[3]).wait_recv()
        w_right_on(a, xs[3]).start()
        w_left(a, xs[1]).wait_recv()
        w_left_on(a, xs[1]).start()

    def w_arrived(a):
        own_w[a].wait()
        w_right_on(a, xs[2]).wait_recv()
        w_left_on(a, xs[2]).wait_recv()

    def w_sent(a):
        for make in (w_right, w_left, w_right_on, w_left_on):
            make(a, r).wait_send()

    ca = CAP // CA

    def z_copy(a, block, k, dev, c):
        ref = rows.at[a, block, pl.ds(c * ca, ca)]
        return remote(ref, ref, zsend.at[a, k, c], zrecv.at[a, block, c], (s, dev, r))

    def z_send(a, k, dev):
        for c in range(CA):
            z_copy(a, e, k, dev, c).start()

    def z_own(a):
        @pl.when(inner)
        def _():
            for c in range(CA):
                z_copy(a, e, 0, other, c).start()
                z_copy(a, e, 1, end, c).start()

        @pl.when(outer)
        def _():
            z_send(a, 0, near)

    def z_pass(a, *moves):
        @pl.when(inner)
        def _():
            for c in range(CA):
                for block, k, dev in moves:
                    copy = z_copy(a, block, k, dev, c)
                    copy.wait_recv()
                    copy.start()

    def normed_rows(pick, tokens):
        x = dot_nn(pick, tokens)
        return (x * inverse_rms(x) * gain_ref[...]).astype(BF)

    smalls[0].wait()
    smalls[1].wait()
    pick_b, pick_scale = slots(be_ref[...], bs_ref[...])
    load_kept.wait()
    smalls[2].wait()
    rows[0, e] = normed_rows(pick_b, kept[...])
    z_own(0)
    smalls[3].wait()
    smalls[4].wait()
    pick_f, _ = slots(fe_ref[...], fs_ref[...])
    z_pass(0, (end, 2, other), (other, 3, end))
    w_pass(0)

    late = s == half - 1
    punctual = jnp.logical_not(late)

    @pl.when(late)
    def _():
        w_pass(1)
        z_pass(0, (far, 4, end))
        hop_inc.wait_recv()
        rows[2, e] = normed_rows(pick_f, inc[...])
        z_own(2)
        out_up()

    @pl.when(s == last)
    def _():
        loss_in.wait()

    @pl.when(s == half - 1)
    def _():
        for k in range(relays):
            in_by(cot, k, half - 1).wait_recv()

    @pl.when(from_next)
    def _():
        hop_cot.wait_recv()

    rows[1, e] = (pick_scale * dot_nn(pick_b, cot[...])).astype(BF)
    z_own(1)

    @pl.when(punctual)
    def _():
        w_pass(1)
        z_pass(0, (far, 4, end))

    pass_relay()

    @pl.when(s == 0)
    def _():
        first_in.wait()

    @pl.when(from_before & punctual)
    def _():
        hop_inc.wait_recv()

    @pl.when(punctual & (s != half))
    def _():
        rows[2, e] = normed_rows(pick_f, inc[...])

    @pl.when(outer & punctual & (s != half))
    def _():
        z_send(2, 0, near)

    z_pass(1, (end, 2, other), (other, 3, end))
    w_pass(2)

    @pl.when(s != half)
    def _():
        z_pass(2, (end, 2, other))

    @pl.when(inner & punctual & (s != half))
    def _():
        z_send(2, 0, other)

    z_pass(1, (far, 4, end))

    @pl.when(s == half)
    def _():
        for k in range(relays):
            in_by(inc, k, half).wait_recv()
        rows[2, e] = normed_rows(pick_f, inc[...])

        @pl.when(outer)
        def _():
            z_send(2, 0, near)

        z_pass(2, (end, 2, other))

        @pl.when(inner)
        def _():
            z_send(2, 0, other)

    def z_arrived(a, block):
        for c in range(CA):
            z_copy(a, block, 0, near, c).wait_recv()

    def project(a, group):
        total = None
        for k in range(4):
            prod = dot_nt(group[:, k * DS : (k + 1) * DS], w[a, k])
            total = prod if total is None else total + prod
        return total

    def backward_acts(group_in, group_grad):
        gate_act = project(0, group_in)
        up_act = project(1, group_in)
        squash = sigmoid(gate_act)
        act = gate_act * squash
        grad_hidden = project(2, group_grad)
        return (
            (grad_hidden * up_act * squash * (1.0 + gate_act * (1.0 - squash))).astype(BF),
            (grad_hidden * act).astype(BF),
            (act * up_act).astype(BF),
        )

    def forward_acts(group):
        g = project(0, group)
        return (g * sigmoid(g) * project(1, group)).astype(BF)

    def backward_part(grad_gate, grad_up, k):
        return (dot_nn(grad_gate, w[0, k]) + dot_nn(grad_up, w[1, k])).astype(BF)

    def forward_part(hidden, k):
        return dot_nn(hidden, w[2, k]).astype(BF)

    def backward_block(block):
        made = backward_acts(rows[0, block], rows[1, block])
        for a in range(3):
            acts[a, block] = made[a]
        for k in range(4):
            part[0, block, :, k * DS : (k + 1) * DS] = backward_part(made[0], made[1], k)

    def forward_block(block):
        hidden = forward_acts(rows[2, block])
        for k in range(4):
            part[1, block, :, k * DS : (k + 1) * DS] = forward_part(hidden, k)

    cr = CAP // CR

    def leg(j, src, dst, k, m, dev, c):
        return remote(src, dst.at[pl.ds(c * cr, cr)], psend.at[j, k, c], precv.at[j, m, c], (s, dev, r))

    def for_far(j, c):
        return leg(j, part.at[j, 3 - e, pl.ds(c * cr, cr)], mid.at[j, 0], 0, 0, near, c)

    def for_across(j, c):
        return leg(j, part.at[j, 3 - near, pl.ds(c * cr, cr)], mid.at[j, 1], 1, 1, near, c)

    def for_near(j, c):
        return leg(j, part.at[j, near, pl.ds(c * cr, cr)], got.at[j, 1], 2, 2, near, c)

    def on_far(j, c):
        return leg(j, part.at[j, far, pl.ds(c * cr, cr)], mid.at[j, 2], 0, 3, other, c)

    def on_other(j, c):
        return leg(j, part.at[j, other, pl.ds(c * cr, cr)], got.at[j, 2], 1, 4, other, c)

    def on_end(j, c):
        return leg(j, part.at[j, end, pl.ds(c * cr, cr)], got.at[j, 1], 2, 2, end, c)

    def add_mid(j, dest, m, c):
        here = pl.ds(c * cr, cr)
        part[j, dest, here, :] = (part[j, dest, here, :].astype(F32) + mid[j, m, here, :].astype(F32)).astype(BF)

    def pass_term(j, dest, m, arriving, leaving):
        for c in range(CR):
            arriving(j, c).wait_recv()
            add_mid(j, dest, m, c)
            leaving(j, c).start()

    def send_term(j, make):
        for c in range(CR):
            make(j, c).start()

    def parts_arrived(j):
        for c in range(CR):
            for_near(j, c).wait_recv()

        @pl.when(inner)
        def _():
            for c in range(CR):
                on_other(j, c).wait_recv()

    def parts_sent(j):
        for k in range(3):
            for c in range(CR):
                leg(j, part.at[j, 0, pl.ds(c * cr, cr)], mid.at[j, 0], k, 0, near, c).wait_send()

    def d_far(a, h):
        half_rows = (up_half, low_half)[h]
        return remote(
            dwst.at[a, xs[2], half_rows], dwmid.at[a, h], dsend.at[a, h], drecv.at[a, h], (right, left)[h]
        )

    def d_near(a, h, joined):
        half_rows = (up_half, low_half)[h if joined else 1 - h]
        n = 2 + 2 * h + (1 if joined else 0)
        return remote(
            dwst.at[a, (xs[1], xs[3])[h], half_rows],
            dwgot.at[a, h, half_rows],
            dsend.at[a, n],
            drecv.at[a, n],
            (right, left)[h],
        )

    def send_weight_grads():
        group_in, group_grad = rows[0].reshape(4 * CAP, D), rows[1].reshape(4 * CAP, D)
        for a, group in enumerate((group_in, group_in, group_grad)):
            act = acts[a].reshape(4 * CAP, HID)
            for k in range(4):
                dwst[a, k] = dot_tt(act, group[:, k * DS : (k + 1) * DS]).astype(BF)
            for h in range(2):
                d_far(a, h).start()

    def send_weight_grads_near():
        for a in range(3):
            for h in range(2):
                d_near(a, h, False).start()

    def join_weight_grads():
        for a in range(3):
            for h in range(2):
                d_far(a, h).wait_recv()
                half_rows, to = (up_half, low_half)[h], (xs[1], xs[3])[h]
                joined = dwst[a, to, half_rows, :].astype(F32) + dwmid[a, h].astype(F32)
                dwst[a, to, half_rows, :] = joined.astype(BF)
                d_near(a, h, True).start()

    gain = gain_ref[...]
    table_b, scale_b = tables(be_ref[...], bs_ref[...])
    table_f, scale_f = tables(fe_ref[...], fs_ref[...])
    rscale_b = inverse_rms(kept[...].astype(F32))

    for a in range(3):
        w_arrived(a)

    gain_z = [remote(gst.at[0, 0], gst.at[0, d], gsend.at[0, d], grecv.at[0, d], (s, zs[d], r)) for d in (1, 2, 3)]
    gain_x = [remote(gst.at[1, 0], gst.at[1, d], gsend.at[1, d], grecv.at[1, d], (s, e, xs[d])) for d in (1, 2, 3)]

    def send_gain():
        terms = part[0].reshape(4 * CAP, D).astype(F32) * rows[0].reshape(4 * CAP, D).astype(F32)
        gst[0, 0] = jnp.sum(terms, axis=0, keepdims=True) / gain
        for c in gain_z:
            c.start()

    def pass_gain():
        for c in gain_z:
            c.wait_recv()
        gst[1, 0] = (gst[0, 0] + gst[0, 1]) + (gst[0, 2] + gst[0, 3])
        for c in gain_x:
            c.start()

    @pl.when(outer)
    def _():
        got[0, 2] = jnp.zeros((CAP, D), BF)
        got[1, 2] = jnp.zeros((CAP, D), BF)
        for block, make in ((near, for_near), (3 - near, for_across), (3 - e, for_far)):
            z_arrived(0, block)
            z_arrived(1, block)
            backward_block(block)
            send_term(0, make)
            if make is for_near:
                backward_block(e)
        send_weight_grads()
        send_gain()
        for block, make in ((3 - e, for_far), (3 - near, for_across), (near, for_near)):
            z_arrived(2, block)
            forward_block(block)
            send_term(1, make)
            if make is for_far:
                send_weight_grads_near()
                forward_block(e)
            if make is for_across:
                join_weight_grads()
                pass_gain()

    @pl.when(inner)
    def _():
        made = backward_acts(rows[0].reshape(4 * CAP, D), rows[1].reshape(4 * CAP, D))
        for a in range(3):
            acts[a] = made[a].reshape(4, CAP, HID)
        for k in range(4):
            part[0, :, :, k * DS : (k + 1) * DS] = backward_part(made[0], made[1], k).reshape(4, CAP, DS)
        send_weight_grads()
        send_gain()

    z_pass(2, (far, 4, end))
    z_pass(2, (other, 3, end))

    @pl.when(inner & punctual)
    def _():
        z_send(2, 1, end)

    @pl.when(inner)
    def _():
        hidden = forward_acts(rows[2].reshape(4 * CAP, D))
        for k in range(4):
            part[1, :, :, k * DS : (k + 1) * DS] = forward_part(hidden, k).reshape(4, CAP, DS)
        send_weight_grads_near()
        pass_term(0, other, 1, for_across, on_other)
        join_weight_grads()
        pass_term(0, far, 0, for_far, on_far)
        pass_gain()
        pass_term(1, far, 0, for_far, on_far)
        pass_term(0, end, 2, on_far, on_end)

    got[0, 0] = part[0, e]
    got[1, 0] = part[1, e]

    parts_arrived(0)
    grad_normed = dot_nn(table_b[:, : 3 * CAP], got[0].reshape(3 * CAP, D))
    xhat = kept[...].astype(F32) * rscale_b
    gx = grad_normed * gain
    mean = jnp.mean(gx * xhat, axis=1, keepdims=True)
    ig[...] = (cot[...].astype(F32) + rscale_b * (gx - xhat * mean)).astype(BF)
    out_ig = pltpu.make_async_copy(ig, ig_ref, osem.at[0])
    out_ig.start()

    @pl.when(inner)
    def _():
        pass_term(1, other, 1, for_across, on_other)
        pass_term(1, end, 2, on_far, on_end)

    outs = [out_ig]
    for a, ref in enumerate((gg_ref, ug_ref, dg_ref)):
        for h in range(2):
            d_near(a, h, False).wait_recv()
            d_near(a, h, True).wait_recv()
        total = dwst[a, r].astype(F32) + (dwgot[a, 0].astype(F32) + dwgot[a, 1].astype(F32))
        dwout[a] = total.astype(BF)
        c = pltpu.make_async_copy(dwout.at[a], ref, osem.at[2 + a])
        c.start()
        outs.append(c)
    parts_arrived(1)
    tokens = dot_nn(table_f[:, : 3 * CAP], got[1].reshape(3 * CAP, D))
    lo[...] = (inc[...].astype(F32) + scale_f * tokens).astype(BF)
    out_lo = pltpu.make_async_copy(lo, lo_ref, osem.at[1])
    out_lo.start()
    outs.append(out_lo)

    for c in gain_x:
        c.wait_recv()
    gout[...] = (gst[1, 0] + gst[1, 1]) + (gst[1, 2] + gst[1, 3])
    c = pltpu.make_async_copy(gout, gt_ref, osem.at[5])
    c.start()
    outs.append(c)

    @pl.when(from_before)
    def _():
        hop_cot.wait_send()

    @pl.when(from_next)
    def _():
        hop_inc.wait_send()

    @pl.when((s == half) | (s == half - 1))
    def _():
        for k in range(relays):
            out_by(so_ref, k, half).wait_send()

    @pl.when(up_relay | down_relay)
    def _():
        in_by(inc, 0, half).wait_send()

    parts_sent(0)
    parts_sent(1)

    for a in range(3):
        w_sent(a)
        for h in range(2):
            d_far(a, h).wait_send()
            d_near(a, h, False).wait_send()
            d_near(a, h, True).wait_send()
    for c in gain_z + gain_x:
        c.wait_send()
    for a in range(3):
        for c in range(CA):
            z_copy(a, e, 0, near, c).wait_send()

        @pl.when(inner)
        def _():
            for k in range(1, 5):
                for c in range(CA):
                    z_copy(a, e, k, end, c).wait_send()

    for c in outs:
        c.wait()


def finish(*refs):
    copies = [pltpu.make_async_copy(refs[i], refs[6 + i], refs[12].at[i]) for i in range(6)]
    for c in copies:
        c.start()
    for c in copies:
        c.wait()


def local(so, ft, kept, sc, lc, gain, gw, uw, dw, fe, fs, be, bs):
    any_spec = pl.BlockSpec(memory_space=pl.ANY)
    dma = pltpu.SemaphoreType.DMA
    hbm = lambda x: pltpu.with_memory_space_constraint(x, pltpu.HBM)
    outs = pl.pallas_call(
        kernel,
        out_shape=(
            jax.ShapeDtypeStruct((TOK, D), BF),
            jax.ShapeDtypeStruct((TOK, D), BF),
            jax.ShapeDtypeStruct((HID, DS), BF),
            jax.ShapeDtypeStruct((HID, DS), BF),
            jax.ShapeDtypeStruct((HID, DS), BF),
            jax.ShapeDtypeStruct((1, D), F32),
        ),
        in_specs=[any_spec] * 13,
        out_specs=[any_spec] * 6,
        scratch_shapes=[
            pltpu.VMEM((TOP, TOK), jnp.int32),
            pltpu.VMEM((TOP, TOK), F32),
            pltpu.VMEM((TOP, TOK), jnp.int32),
            pltpu.VMEM((TOP, TOK), F32),
            pltpu.VMEM((1, D), F32),
            pltpu.VMEM((TOK, D), BF),
            pltpu.VMEM((TOK, D), BF),
            pltpu.VMEM((TOK, D), BF),
            pltpu.VMEM((3, 4, HID, DS), BF),
            pltpu.VMEM((3, 4, CAP, D), BF),
            pltpu.VMEM((2, 4, CAP, D), BF),
            pltpu.VMEM((2, 3, CAP, D), BF),
            pltpu.VMEM((2, 3, CAP, D), BF),
            pltpu.VMEM((16, D), BF),
            pltpu.VMEM((3, 4, CAP, HID), BF),
            pltpu.VMEM((3, 4, HID, DS), BF),
            pltpu.VMEM((3, 2, HID // 2, DS), BF),
            pltpu.VMEM((3, 2, HID, DS), BF),
            pltpu.VMEM((3, HID, DS), BF),
            pltpu.VMEM((TOK, D), BF),
            pltpu.VMEM((TOK, D), BF),
            pltpu.VMEM((2, 4, 1, D), F32),
            pltpu.VMEM((1, D), F32),
            dma((11,)),
            dma((6,)),
            dma((2,)),
            dma((2,)),
            dma((3, 4)),
            dma((3, 4)),
            dma((3, 5, CA)),
            dma((3, 4, CA)),
            dma((2, 3, CR)),
            dma((2, 5, CR)),
            dma((8,)),
            dma((8,)),
            dma((2,)),
            pltpu.SemaphoreType.REGULAR,
            dma((3, 6)),
            dma((3, 6)),
            dma((2, 4)),
            dma((2, 4)),
        ],
        compiler_params=pltpu.CompilerParams(
            collective_id=0, has_side_effects=True, vmem_limit_bytes=40 << 20
        ),
        name="relay",
    )(
        hbm(so.reshape(TOK, D)), hbm(ft.reshape(TOK, D)), hbm(kept.reshape(TOK, D)), hbm(sc.reshape(TOK, D)),
        hbm(lc.reshape(TOK, D)), hbm(gain.reshape(1, D)), hbm(gw[0]), hbm(uw[0]), hbm(dw[0]),
        hbm(fe[0, 0].T), hbm(fs[0, 0].T), hbm(be[0, 0].T), hbm(bs[0, 0].T),
    )
    outs = pl.pallas_call(
        finish,
        out_shape=tuple(jax.ShapeDtypeStruct(o.shape, o.dtype) for o in outs),
        in_specs=[any_spec] * 6,
        out_specs=[any_spec] * 6,
        scratch_shapes=[dma((6,))],
        compiler_params=pltpu.CompilerParams(vmem_limit_bytes=16 << 20),
        name="finish",
    )(*[pltpu.with_memory_space_constraint(o, pltpu.VMEM) for o in outs])
    return (
        outs[0][None, None], outs[1][None, None], outs[2][None], outs[3][None], outs[4][None], outs[5],
    )


def solution(mesh):
    tokens = P("section", "dp", "expert", None)
    stored = P("section", "expert", "dp")
    first = P("dp", "expert", None)
    return jax.shard_map(
        local,
        mesh=mesh,
        in_specs=(tokens, first, tokens, tokens, first, P("section", None)) + (stored,) * 3 + (tokens,) * 4,
        out_specs=(tokens, tokens, stored, stored, stored, P("section", None)),
        check_vma=False,
    )
```
